32 devices in a mesh: seq: 4 (over z), fsdp: 8 (over y, x, core).
Axes of the slice: x: 2, y: 2, z: 4, core: 2. Of those that a mesh axis runs over, the one named last changes fastest.
Arguments:
- tokens: bfloat16 [8, 3072, 768], P('fsdp', 'seq'), may hold values from -6 to 6
- w_qkv: bfloat16 [768, 2304], P('fsdp'), may hold values from -0.21875 to 0.21875
- w_out: bfloat16 [768, 768], P('fsdp'), may hold values from -6 to 6
- w_in: bfloat16 [768, 2304], P('fsdp'), may hold values from -0.21875 to 0.21875
- w_down: bfloat16 [1152, 768], P('fsdp'), may hold values from -0.1875 to 0.1875
- gain_attn: bfloat16 [768], P('fsdp'), may hold values from 0.5 to 1.5
- gain_mlp: bfloat16 [768], P('fsdp'), may hold values from 0.5 to 1.5
- lengths: int32 [8], P('fsdp'), may hold values from 2305 to 3072, as said below
- cotangent: bfloat16 [8, 3072, 768], P('fsdp', 'seq'), may hold values from -6 to 6
Outputs:
- layer_out: bfloat16 [8, 3072, 768], P('fsdp', 'seq')
- grad_tokens: bfloat16 [8, 3072, 768], P('fsdp', 'seq')
- grad_w_qkv: float32 [768, 2304], P('fsdp')
- grad_w_out: float32 [768, 768], P('fsdp')
- grad_w_in: float32 [768, 2304], P('fsdp')
- grad_w_down: float32 [1152, 768], P('fsdp')
- grad_gain_attn: float32 [768], P('fsdp')
- grad_gain_mlp: float32 [768], P('fsdp')
The draws below stay inside these ranges and needn't reach their ends.
Inputs may be any that keep to these rules, and one draw needn't show every extreme that they name: lengths[s] is the number of valid tokens of sequence s; positions at or beyond it are padding, masked as keys. Some sequence has all 3072 valid in every draw.
All inputs are finite; a program needn't handle non-finite values.
Results may differ from the reference program's by a relative error of at most 0.015.
Values may be sent and summed in bfloat16 or wider, within the bound.
No kernel may reach another device: no remote copies, remote signals or barrier semaphores. Data moves between devices by JAX's collectives and lax.ppermute only.
A program may use at most 128 MiB of HBM per device.

```python
import math
import jax
import jax.numpy as jnp
from jax import lax

D = 768
HEADS = 12
FF = 1152
LEN = 3072
SEQS = 8


def draw_lengths(key, part):
    key = jax.random.fold_in(key, 11)
    pick_key, value_key = jax.random.split(key)
    values = jax.random.randint(value_key, (SEQS,), 3 * LEN // 4 + 1, LEN + 1)
    chosen = jax.random.randint(pick_key, (), 0, SEQS)
    return jnp.where(jnp.arange(SEQS) == chosen, LEN, values).astype(jnp.int32)


def block_levels(rng, extent, shards, least, top_value):
    factor_of, own = 1.0, jax.random.fold_in(rng, 6)
    for dim, shards_of in shards:
        draws = jnp.exp(jax.random.uniform(jax.random.fold_in(own, dim), (shards_of,), jnp.float32, least / len(shards), top_value / len(shards)))
        factor_of = factor_of * jnp.repeat(draws, extent[dim] // shards_of).reshape([-1 if axis == dim else 1 for axis in range(len(extent))])
    return factor_of


def scatter_about(rng, dims, scale, bound, cuts=(), dtype=jnp.bfloat16):
    drawn = jax.random.normal(rng, dims, jnp.float32) * scale
    if len(cuts) > 0:
        drawn = block_levels(rng, dims, cuts, -0.22, 0.18) * drawn
    return jnp.clip(drawn, min=-bound, max=bound).astype(dtype)


def setup_inputs(seed: int = 0) -> dict:
    seeds = jax.random.split(jax.random.key(seed), 10)
    return {
        "tokens": scatter_about(seeds[0], (SEQS, LEN, D), 1.0, 6.0, ((0, 8), (1, 4))),
        "w_qkv": scatter_about(seeds[1], (D, 3 * D), D ** -0.5, 0.21875, ((0, 8),)),
        "w_out": scatter_about(seeds[2], (D, D), (max(1, 4 * D // LEN)) ** -0.5, 6.0, ((0, 8),)),
        "w_in": scatter_about(seeds[3], (D, 2 * FF), D ** -0.5, 0.21875, ((0, 8),)),
        "w_down": scatter_about(seeds[4], (FF, D), FF ** -0.5, 0.1875, ((0, 8),)),
        "gain_attn": jnp.clip(1.0 + 0.1 * jax.random.normal(seeds[5], (D,), jnp.float32), 0.5, 1.5).astype(jnp.bfloat16),
        "gain_mlp": jnp.clip(1.0 + 0.1 * jax.random.normal(seeds[6], (D,), jnp.float32), 0.5, 1.5).astype(jnp.bfloat16),
        "lengths": draw_lengths(jax.random.fold_in(seeds[9], 71), 0),
        "cotangent": scatter_about(seeds[8], (SEQS, LEN, D), 1.0, 6.0, ((0, 8), (1, 4))),
    }


norm_eps = 1e-05
rope_base = 160000.0
masked_score = -1e+30
highest = lax.Precision.HIGHEST

@jax.custom_vjp
def low(v):
    return lax.optimization_barrier(v.astype(jnp.bfloat16)).astype(jnp.float32)

@jax.custom_vjp
def low_back(v):
    return v

def low_keep(v):
    return (low(v), None)

def low_pass(kept, grad):
    return (grad,)

def back_keep(v):
    return (v, None)

def back_low(kept, grad):
    return (low(grad),)
low.defvjp(low_keep, low_pass)
low_back.defvjp(back_keep, back_low)

def normalize(values, gain):
    centre = values - lax.optimization_barrier(jnp.mean(values, -1, keepdims=True))
    spread = lax.optimization_barrier(jnp.mean(centre * centre, -1, keepdims=True))
    return centre * lax.rsqrt(spread + norm_eps) * gain

def rotary(positions, half_dim):
    counter = jnp.arange(half_dim).astype(jnp.float32)
    inverse = jnp.exp(counter * (-math.log(rope_base) / half_dim))
    angles = positions[:, None] * inverse[None, :]
    return (jnp.cos(angles), jnp.sin(angles))

def turn(values, cosine, sine):
    half_dim = values.shape[-1] // 2
    lower = values[..., :half_dim]
    upper = values[..., half_dim:]
    return jnp.concatenate([lower * cosine - upper * sine, upper * cosine + lower * sine], -1)

def geglu(gate, upper):
    return jax.nn.gelu(gate, approximate=False) * upper

def sequence(inputs, length, w_qkv, w_out, w_in, w_down, gain_attn, gain_mlp, cosine, sine):
    tok_rows, width = inputs.shape
    head_dim = width // HEADS
    scale = head_dim ** (-0.5)
    h_first = low(normalize(inputs, gain_attn))
    joined = low_back(jnp.dot(h_first, w_qkv, precision=highest)).reshape(tok_rows, 3, HEADS, head_dim)
    query = low(low_back(turn(joined[:, 0], cosine[:, None, :], sine[:, None, :])))
    key_all = low(low_back(turn(joined[:, 1], cosine[:, None, :], sine[:, None, :])))
    value = low(low_back(joined[:, 2]))
    valid = jnp.arange(tok_rows) < length
    block_rows = min(512, tok_rows)
    query_blocks = query.reshape(tok_rows // block_rows, block_rows, HEADS, head_dim)

    def attend(query_block):
        score = low_back(jnp.einsum('qhd,khd->hqk', query_block, key_all, precision=highest) * scale)
        score = jnp.where(valid[None, None, :], score, masked_score)
        rowmax = lax.optimization_barrier(jnp.max(score, -1, keepdims=True))
        expo = jnp.exp(score - rowmax)
        prob = low(low_back(expo / lax.optimization_barrier(jnp.sum(expo, -1, keepdims=True))))
        return low(low_back(jnp.einsum('hqk,khd->qhd', prob, value, precision=highest)))
    mixed = lax.map(jax.checkpoint(attend), query_blocks).reshape(tok_rows, width)
    resid = inputs + low_back(jnp.dot(mixed, w_out, precision=highest))
    h_second = low(normalize(resid, gain_mlp))
    gate_up = low_back(jnp.dot(h_second, w_in, precision=highest))
    width_ff = gate_up.shape[1] // 2
    act = low(geglu(gate_up[:, :width_ff], gate_up[:, width_ff:]))
    return resid + jnp.dot(act, w_down, precision=highest)

def forward(inputs, w_qkv, w_out, w_in, w_down, gain_attn, gain_mlp, lengths):
    tok_rows = inputs.shape[1]
    head_dim = inputs.shape[2] // HEADS
    cosine, sine = rotary(jnp.arange(tok_rows).astype(jnp.float32), head_dim // 2)

    def step(carry, item):
        one_seq, length = item
        return (carry, sequence(one_seq, length, w_qkv, w_out, w_in, w_down, gain_attn, gain_mlp, cosine, sine))
    _, outputs = lax.scan(step, jnp.zeros((), jnp.float32), (inputs, lengths))
    return outputs

def reference(tokens, w_qkv, w_out, w_in, w_down, gain_attn, gain_mlp, lengths, cotangent):

    def wrapped(inputs, wa, wb, wc, wd, ga, gb):
        return forward(inputs, wa, wb, wc, wd, ga, gb, lengths)
    primal, pullback = jax.vjp(wrapped, tokens.astype(jnp.float32), w_qkv.astype(jnp.float32), w_out.astype(jnp.float32), w_in.astype(jnp.float32), w_down.astype(jnp.float32), gain_attn.astype(jnp.float32), gain_mlp.astype(jnp.float32))
    grads = pullback(cotangent.astype(jnp.float32))
    return (primal.astype(jnp.bfloat16), grads[0].astype(jnp.bfloat16), grads[1], grads[2], grads[3], grads[4], grads[5], grads[6])
```

```python
import functools
import math

import jax
import jax.numpy as jnp
from jax import lax
from jax.experimental import pallas as pl
from jax.experimental.pallas import tpu as pltpu
from jax.sharding import PartitionSpec as P

HEADS = 12


norm_eps = 1e-05
rope_base = 160000.0
masked_score = -1e30
LANES = 128
EVERY = ("zp", "zi", "chip", "core")
VMEM = 56 << 20


def dot(left, right, left_dim=1, right_dim=0):
    return lax.dot_general(
        left,
        right,
        (((left_dim,), (right_dim,)), ((), ())),
        preferred_element_type=jnp.float32,
    )


def call(kernel, grid, in_specs, out_specs, out_shape, scratch, flops, moved, exps=0):
    return pl.pallas_call(
        kernel,
        grid=grid,
        in_specs=in_specs,
        out_specs=out_specs,
        out_shape=out_shape,
        scratch_shapes=scratch,
        cost_estimate=pl.CostEstimate(flops=flops, bytes_accessed=moved, transcendentals=exps),
        compiler_params=pltpu.CompilerParams(vmem_limit_bytes=VMEM),
    )


def shape(dims, dtype):
    return jax.ShapeDtypeStruct(dims, dtype)


def rotary_tables(positions, half_dim):
    counter = jnp.arange(half_dim).astype(jnp.float32)
    inverse = jnp.exp(counter * (-math.log(rope_base) / half_dim))
    angles = positions[:, None] * inverse[None, :]
    cosine, sine = jnp.cos(angles), jnp.sin(angles)
    return (
        jnp.concatenate([cosine] * 4, -1),
        jnp.concatenate([-sine, sine, -sine, sine], -1),
    )


def swap_halves(values, head_dim):
    half = head_dim // 2
    lane = lax.broadcasted_iota(jnp.int32, values.shape, 1)
    ahead = pltpu.roll(values, LANES - half, 1)
    behind = pltpu.roll(values, half, 1)
    return jnp.where(lane % head_dim < half, ahead, behind)


def project_kernel(tiles, head_dim, own, other, gain, weight, cosine, sine, h_out, q_out, *kv_out):
    step = pl.program_id(0)
    values = jnp.where(step < tiles, own[...], other[...]).astype(jnp.float32)
    centre = values - jnp.mean(values, -1, keepdims=True)
    spread = jnp.mean(centre * centre, -1, keepdims=True)
    hidden = (centre * lax.rsqrt(spread + norm_eps) * gain[...]).astype(jnp.bfloat16)
    h_out[...] = hidden
    joined = dot(hidden, weight[...])
    width = q_out.shape[1]
    cos, sin = cosine[...], sine[...]
    factor = head_dim ** (-0.5) * math.log2(math.e)
    for pair in range(width // LANES):
        at = pair * LANES
        query = joined[:, at : at + LANES]
        query = query * cos + swap_halves(query, head_dim) * sin
        q_out[:, at : at + LANES] = (query * factor).astype(jnp.bfloat16)
        key = joined[:, width + at : width + at + LANES]
        key = key * cos + swap_halves(key, head_dim) * sin
        kv_out[pair][:, :LANES] = key.astype(jnp.bfloat16)
        value = joined[:, 2 * width + at : 2 * width + at + LANES]
        kv_out[pair][:, LANES:] = value.astype(jnp.bfloat16)


def project(own, other, gain, weight, cosine, sine, head_dim):
    rows, depth = own.shape
    block = 256
    tiles = rows // block
    width = weight.shape[1] // 3
    pairs = width // LANES
    by_row = lambda step: (step, 0)
    whole = lambda step: (0, 0)
    return call(
        functools.partial(project_kernel, tiles, head_dim),
        (2 * tiles,),
        [
            pl.BlockSpec((block, depth), lambda step: (jnp.minimum(step, tiles - 1), 0)),
            pl.BlockSpec((block, depth), lambda step: (jnp.maximum(step - tiles, 0), 0)),
            pl.BlockSpec((1, depth), whole),
            pl.BlockSpec(weight.shape, whole),
            pl.BlockSpec((block, LANES), by_row),
            pl.BlockSpec((block, LANES), by_row),
        ],
        [pl.BlockSpec((block, depth), by_row), pl.BlockSpec((block, width), by_row)]
        + [pl.BlockSpec((block, 2 * LANES), by_row)] * pairs,
        [shape((2 * rows, depth), jnp.bfloat16), shape((2 * rows, width), jnp.bfloat16)]
        + [shape((2 * rows, 2 * LANES), jnp.bfloat16)] * pairs,
        [],
        2 * 2 * rows * depth * 3 * width,
        2 * rows * (2 * depth + 3 * width) * 2 + weight.size * 2,
    )(own, other, gain, weight, cosine, sine)


def attend_kernel(head_dim, sources, first, last, *refs):
    refs = list(refs)
    query = refs.pop(0)
    keys = [(refs.pop(0), refs.pop(0)) for _ in range(sources)]
    if not first:
        acc_in, max_in = refs.pop(0), refs.pop(0)
    if last:
        mixed, log_total = refs.pop(0), refs.pop(0)
    else:
        acc_out, max_out = refs.pop(0), refs.pop(0)
    key_of, value_of, bias_of = refs
    span = keys[0][0].shape[0]

    @pl.when(pl.program_id(0) == 0)
    def prepare():
        low = lax.broadcasted_iota(jnp.int32, (span, LANES), 1) < head_dim
        one = jnp.ones((span, LANES), jnp.bfloat16)
        zero = jnp.zeros((span, LANES), jnp.bfloat16)
        for source, (key_value, bias) in enumerate(keys):
            part = pl.ds(source * span, span)
            key, value = key_value[:, :LANES], key_value[:, LANES:]
            key_of[0, part, :] = jnp.where(low, key, zero)
            key_of[1, part, :] = jnp.where(low, zero, key)
            value_of[0, part, :] = jnp.where(low, value, one)
            value_of[1, part, :] = jnp.where(low, one, value)
            bias_of[:, part] = bias[...]

    low = lax.broadcasted_iota(jnp.int32, (query.shape[0], LANES), 1) < head_dim
    held = query[...]
    results, tops = [], []
    for head in range(2):
        score = dot(held, key_of[head], 1, 1) + bias_of[...]
        top = jnp.max(score, 1, keepdims=True)
        if not first:
            before = max_in[:, head * head_dim : head * head_dim + 1]
            top = jnp.maximum(top, before)
        expo = jnp.exp2(score - top).astype(jnp.bfloat16)
        result = dot(expo, value_of[head])
        if not first:
            result = result + acc_in[:, head * LANES : (head + 1) * LANES] * jnp.exp2(before - top)
        results.append(result)
        tops.append(top)
    top = jnp.where(low, tops[0], tops[1])
    if last:
        total = jnp.where(
            low, pltpu.roll(results[0], head_dim, 1), pltpu.roll(results[1], head_dim, 1)
        )
        mixed[...] = (jnp.where(low, results[0], results[1]) / total).astype(mixed.dtype)
        log_total[...] = top + jnp.log2(total)
    else:
        acc_out[:, :LANES] = results[0]
        acc_out[:, LANES:] = results[1]
        max_out[...] = top


def attend(query, pair, keys, state=None, last=True, head_dim=64):
    rows = query.shape[0]
    span = keys[0][0].shape[0]
    block = min(512, rows)
    by_row = lambda step: (step, 0)
    whole = lambda step: (0, 0)
    narrow = pl.BlockSpec((block, LANES), by_row)
    wide = pl.BlockSpec((block, 2 * LANES), by_row)
    in_specs = [pl.BlockSpec((block, LANES), lambda step: (step, pair))]
    args = [query]
    for key_value, bias in keys:
        in_specs += [pl.BlockSpec((span, 2 * LANES), whole), pl.BlockSpec((1, span), whole)]
        args += [key_value, bias]
    if state is not None:
        in_specs += [wide, narrow]
        args += list(state)
    if last:
        out_specs = [narrow, narrow]
        out_shape = [shape((rows, LANES), jnp.bfloat16), shape((rows, LANES), jnp.float32)]
    else:
        out_specs = [wide, narrow]
        out_shape = [shape((rows, 2 * LANES), jnp.float32), shape((rows, LANES), jnp.float32)]
    count = span * len(keys)
    return call(
        functools.partial(attend_kernel, head_dim, len(keys), state is None, last),
        (rows // block,),
        in_specs,
        out_specs,
        out_shape,
        [
            pltpu.VMEM((2, count, LANES), jnp.bfloat16),
            pltpu.VMEM((2, count, LANES), jnp.bfloat16),
            pltpu.VMEM((1, count), jnp.float32),
        ],
        2 * 2 * 2 * rows * count * 256,
        rows * LANES * 8 + count * 512,
        2 * rows * count,
    )(*args)


def revisit_kernel(
    head_dim, key_value, bias, query, mixed, grad, log_total, dq_out, dkv_out,
    grad_key, grad_value, key_of, value_of,
):
    span = key_value.shape[0]
    step = pl.program_id(0)

    @pl.when(step == 0)
    def prepare():
        low = lax.broadcasted_iota(jnp.int32, (span, LANES), 1) < head_dim
        zero = jnp.zeros((span, LANES), jnp.bfloat16)
        key, value = key_value[:, :LANES], key_value[:, LANES:]
        key_of[0] = jnp.where(low, key, zero)
        key_of[1] = jnp.where(low, zero, key)
        value_of[0] = jnp.where(low, value, zero)
        value_of[1] = jnp.where(low, zero, value)
        grad_key[...] = jnp.zeros_like(grad_key)
        grad_value[...] = jnp.zeros_like(grad_value)

    rows = query.shape[0]
    block = min(256, rows)
    for start in range(0, rows, block):
        part = pl.ds(start, block)
        held, back = query[part, :], grad[part, :]
        held_t, back_t = held.T, back.T
        product = back.astype(jnp.float32) * mixed[part, :].astype(jnp.float32)
        grad_query = None
        for head in range(2):
            lanes = slice(head * head_dim, (head + 1) * head_dim)
            weighted = jnp.sum(product[:, lanes], 1, keepdims=True)
            log_block = log_total[part, head * head_dim : head * head_dim + 1]
            prob = jnp.exp2(dot(held, key_of[head], 1, 1) + bias[...] - log_block)
            grad_prob = dot(back, value_of[head], 1, 1)
            grad_score = (prob * (grad_prob - weighted)).astype(jnp.bfloat16)
            grad_value[lanes, :] += dot(back_t[lanes], prob.astype(jnp.bfloat16))
            grad_key[lanes, :] += dot(held_t[lanes], grad_score)
            term = dot(grad_score, key_of[head])
            grad_query = term if grad_query is None else grad_query + term
        dq_out[part, :] = grad_query * head_dim ** (-0.5)

    @pl.when(step == pl.num_programs(0) - 1)
    def finish():
        dkv_out[:, :LANES] = (grad_key[...].T * math.log(2.0)).astype(dkv_out.dtype)
        dkv_out[:, LANES:] = grad_value[...].T.astype(dkv_out.dtype)


def revisit(query, pair, key_value, bias, mixed, grad, log_total, head_dim=64):
    rows = query.shape[0]
    span = key_value.shape[0]
    block = min(512, rows)
    by_row = lambda step: (step, 0)
    by_pair = lambda step: (step, pair)
    whole = lambda step: (0, 0)
    narrow = pl.BlockSpec((block, LANES), by_row)
    return call(
        functools.partial(revisit_kernel, head_dim),
        (rows // block,),
        [
            pl.BlockSpec((span, 2 * LANES), whole),
            pl.BlockSpec((1, span), whole),
            pl.BlockSpec((block, LANES), by_pair),
            narrow,
            pl.BlockSpec((block, LANES), by_pair),
            narrow,
        ],
        [narrow, pl.BlockSpec((span, 2 * LANES), whole)],
        [shape((rows, LANES), jnp.float32), shape((span, 2 * LANES), jnp.bfloat16)],
        [
            pltpu.VMEM((LANES, span), jnp.float32),
            pltpu.VMEM((LANES, span), jnp.float32),
            pltpu.VMEM((2, span, LANES), jnp.bfloat16),
            pltpu.VMEM((2, span, LANES), jnp.bfloat16),
        ],
        5 * 2 * 2 * rows * span * 200,
        rows * LANES * 14 + span * 1024,
        2 * rows * span,
    )(key_value, bias, query, mixed, grad, log_total)


def unproject_kernel(pairs, head_dim, *refs):
    refs = list(refs)
    hidden, weight, cosine, sine = refs[:4]
    refs = refs[4:]
    near_q, far_q = refs[:pairs], refs[pairs : 2 * pairs]
    near_kv, far_kv = refs[2 * pairs : 3 * pairs], refs[3 * pairs : 4 * pairs]
    dh_out, dw_out, joined, total = refs[4 * pairs :]
    step = pl.program_id(0)
    width = pairs * LANES
    cos, sin = cosine[...], sine[...]
    for pair in range(pairs):
        at = pair * LANES
        query = near_q[pair][...] + far_q[pair][...]
        query = query * cos - swap_halves(query, head_dim) * sin
        joined[:, at : at + LANES] = query.astype(jnp.bfloat16)
        both = near_kv[pair][...].astype(jnp.float32) + far_kv[pair][...].astype(jnp.float32)
        key, value = both[:, :LANES], both[:, LANES:]
        key = key * cos - swap_halves(key, head_dim) * sin
        joined[:, width + at : width + at + LANES] = key.astype(jnp.bfloat16)
        joined[:, 2 * width + at : 2 * width + at + LANES] = value.astype(jnp.bfloat16)
    dh_out[...] = dot(joined[...], weight[...], 1, 1).astype(dh_out.dtype)
    share = dot(hidden[...], joined[...], 0, 0)

    @pl.when(step == 0)
    def begin():
        total[...] = share

    @pl.when(step > 0)
    def add():
        total[...] += share

    @pl.when(step == pl.num_programs(0) - 1)
    def finish():
        dw_out[...] = total[...].astype(dw_out.dtype)


def unproject(hidden, weight, cosine, sine, near_q, far_q, near_kv, far_kv, head_dim):
    rows, depth = hidden.shape
    block = 256
    pairs = len(near_q)
    by_row = lambda step: (step, 0)
    whole = lambda step: (0, 0)
    narrow = pl.BlockSpec((block, LANES), by_row)
    wide = pl.BlockSpec((block, 2 * LANES), by_row)
    return call(
        functools.partial(unproject_kernel, pairs, head_dim),
        (rows // block,),
        [pl.BlockSpec((block, depth), by_row), pl.BlockSpec(weight.shape, whole), narrow, narrow]
        + [narrow] * (2 * pairs)
        + [wide] * (2 * pairs),
        [pl.BlockSpec((block, depth), by_row), pl.BlockSpec(weight.shape, whole)],
        [shape((rows, depth), jnp.bfloat16), shape(weight.shape, jnp.bfloat16)],
        [pltpu.VMEM((block, weight.shape[1]), jnp.bfloat16), pltpu.VMEM(weight.shape, jnp.float32)],
        4 * rows * weight.size,
        rows * (depth * 4 + pairs * LANES * 16) + weight.size * 4,
    )(hidden, weight, cosine, sine, *near_q, *far_q, *near_kv, *far_kv)


def position(axes):
    place = 0
    for axis in axes:
        place = place * lax.axis_size(axis) + lax.axis_index(axis)
    return place


def others(axes):
    count = math.prod(lax.axis_size(axis) for axis in axes)
    return count, [
        [(source, source ^ step) for source in range(count)] for step in range(1, count)
    ]


def gather(block, axes):
    count, steps = others(axes)
    if count > 4:
        return lax.all_gather(block, axes, axis=0, tiled=True)
    place = position(axes)
    rows = block.shape[0]
    whole = jnp.zeros((count * rows,) + block.shape[1:], block.dtype)
    parts = [block] + [lax.ppermute(block, axes, pairs) for pairs in steps]
    for step, part in enumerate(parts):
        whole = lax.dynamic_update_slice_in_dim(whole, part, (place ^ step) * rows, 0)
    return whole


def scatter_sum(whole, axes):
    count, steps = others(axes)
    if count > 4:
        return lax.psum_scatter(whole, axes, scatter_dimension=0, tiled=True).astype(jnp.float32)
    place = position(axes)
    rows = whole.shape[0] // count
    total = lax.dynamic_slice_in_dim(whole, place * rows, rows, 0).astype(jnp.float32)
    for step, pairs in enumerate(steps, 1):
        block = lax.dynamic_slice_in_dim(whole, (place ^ step) * rows, rows, 0)
        total = total + lax.ppermute(block, axes, pairs).astype(jnp.float32)
    return total


def full_sum(values, axes):
    count, steps = others(axes)
    if count > 4:
        return lax.psum(values, axes)
    return values + sum(lax.ppermute(values, axes, pairs) for pairs in steps)


def core_swap(block):
    return lax.ppermute(block, "core", [(0, 1), (1, 0)])


def normalize(values, gain):
    centre = values - jnp.mean(values, -1, keepdims=True)
    spread = jnp.mean(centre * centre, -1, keepdims=True)
    return centre * lax.rsqrt(spread + norm_eps) * gain


def geglu(gate, upper):
    return jax.nn.gelu(gate, approximate=False) * upper


def shards(tokens, w_qkv, w_out, w_in, w_down, gain_attn, gain_mlp, lengths, cotangent):
    rows, width = tokens.shape[1:]
    head_dim = width // HEADS
    half = width // 2
    pairs = half // LANES
    chips = lax.axis_size("chip")
    core, inner = lax.axis_index("core"), lax.axis_index("zi")
    first_core = core == 0
    seq_axes = ("zp", "zi")
    low = jnp.bfloat16

    places = [(zp, zi, chip, c) for zp in range(2) for zi in range(2) for chip in range(chips) for c in range(2)]
    number = {place: index for index, place in enumerate(places)}
    move = [(number[(zp, zi, chip, c)], number[(c, zi, chip, zp)]) for zp, zi, chip, c in places]
    own = lax.ppermute(tokens[0], EVERY, move)
    length = lax.ppermute(lengths, EVERY, move)[0]
    grad_out = lax.ppermute(cotangent[0], EVERY, move)
    other = core_swap(own)

    shard = w_qkv.shape[0]
    by_core = w_qkv.reshape(shard, 3, 2, half)
    kept = jnp.where(first_core, by_core[:, :, 0], by_core[:, :, 1]).reshape(shard, 3 * half)
    given = jnp.where(first_core, by_core[:, :, 1], by_core[:, :, 0]).reshape(shard, 3 * half)
    taken = core_swap(given)
    weight = jnp.where(
        first_core, jnp.concatenate([kept, taken], 0), jnp.concatenate([taken, kept], 0)
    )
    weight = gather(weight, ("chip",))
    gains = jnp.stack([gain_attn, gain_mlp], 1)
    gains = jnp.concatenate([gains, core_swap(gains)], 0)
    gains = jnp.where(first_core, gains, jnp.roll(gains, shard, 0))
    gains = gather(gains, ("chip",)).astype(jnp.float32)
    first_gain, second_gain = gains[:, 0], gains[:, 1]

    m_out = lax.all_gather(w_out, ("chip", "core"), axis=0, tiled=True)
    m_in = lax.all_gather(w_in, ("chip", "core"), axis=0, tiled=True)
    m_down = lax.all_gather(w_down, ("chip", "core"), axis=0, tiled=True)

    steps = jnp.arange(rows)
    own_at = (2 * core + inner) * rows + steps
    other_at = (2 * (1 - core) + inner) * rows + steps
    here = jnp.concatenate([own_at, other_at])
    there = here + jnp.where(inner == 0, rows, -rows)
    cosine, sine = rotary_tables(here.astype(jnp.float32), head_dim // 2)
    near_bias = jnp.where(here < length, 0.0, masked_score).astype(jnp.float32)[None]
    far_bias = jnp.where(there < length, 0.0, masked_score).astype(jnp.float32)[None]

    hidden, query, *near = project(
        own, other, first_gain[None], weight, cosine, sine, head_dim
    )
    swap_chips = [(0, 1), (1, 0)]
    far = [lax.ppermute(key_value, "zi", swap_chips) for key_value in near]
    state = attend(query, pairs - 1, [(near[-1], near_bias)], last=False)
    attended = [
        attend(query, pair, [(near[pair], near_bias), (far[pair], far_bias)])
        for pair in range(pairs - 1)
    ]
    attended.append(attend(query, pairs - 1, [(far[-1], far_bias)], state))

    mine = jnp.concatenate([mixed[:rows] for mixed, _ in attended], 1)
    theirs = core_swap(jnp.concatenate([mixed[rows:] for mixed, _ in attended], 1))
    mixed = jnp.where(
        first_core, jnp.concatenate([mine, theirs], 1), jnp.concatenate([theirs, mine], 1)
    )

    inputs = own.astype(jnp.float32)
    resid = inputs + dot(mixed, m_out)
    h_second, second_norm_back = jax.vjp(normalize, resid, second_gain)
    h_second_low = h_second.astype(low)
    gate_up = dot(h_second_low, m_in)
    width_ff = gate_up.shape[1] // 2
    act, act_back = jax.vjp(geglu, gate_up[:, :width_ff], gate_up[:, width_ff:])
    act_low = act.astype(low)
    layer_out = (resid + dot(act_low, m_down)).astype(low)

    grad_down = dot(act_low, grad_out, 0, 0).astype(low)
    grad_act = dot(grad_out, m_down, 1, 1)
    grad_gate, grad_upper = act_back(grad_act)
    grad_gate_up = jnp.concatenate([grad_gate, grad_upper], 1).astype(low)
    grad_in = dot(h_second_low, grad_gate_up, 0, 0).astype(low)
    grad_h_second = dot(grad_gate_up, m_in, 1, 1)
    grad_resid_norm, grad_second_gain = second_norm_back(grad_h_second)
    grad_resid = grad_out.astype(jnp.float32) + grad_resid_norm
    grad_attn = grad_resid.astype(low)
    grad_wout = dot(mixed, grad_attn, 0, 0).astype(low)
    grad_mixed = dot(grad_attn, m_out, 1, 1).astype(low)

    kept = jnp.where(first_core, grad_mixed[:, :half], grad_mixed[:, half:])
    given = jnp.where(first_core, grad_mixed[:, half:], grad_mixed[:, :half])
    back = jnp.concatenate([kept, core_swap(given)], 0)

    far_grads = [
        revisit(query, pair, far[pair], far_bias, attended[pair][0], back, attended[pair][1])
        for pair in range(pairs)
    ]
    returned = [lax.ppermute(grads[1], "zi", swap_chips) for grads in far_grads]
    near_grads = [
        revisit(query, pair, near[pair], near_bias, attended[pair][0], back, attended[pair][1])
        for pair in range(pairs)
    ]
    grad_hidden, grad_weight = unproject(
        hidden,
        weight,
        cosine,
        sine,
        [grads[0] for grads in near_grads],
        [grads[0] for grads in far_grads],
        [grads[1] for grads in near_grads],
        returned,
        head_dim,
    )

    grad_h_first = grad_hidden[:rows].astype(jnp.float32) + core_swap(grad_hidden[rows:]).astype(
        jnp.float32
    )
    _, first_norm_back = jax.vjp(normalize, inputs, first_gain)
    grad_input_norm, grad_first_gain = first_norm_back(grad_h_first)
    grad_tokens = (grad_resid + grad_input_norm).astype(low)

    total = scatter_sum(grad_weight, ("chip",)).astype(low)
    total = gather(scatter_sum(total, seq_axes), seq_axes)
    kept = jnp.where(first_core, total[:shard], total[shard:])
    given = jnp.where(first_core, total[shard:], total[:shard])
    taken = core_swap(given)
    total_qkv = jnp.where(
        first_core, jnp.stack([kept, taken], 1), jnp.stack([taken, kept], 1)
    ).reshape(shard, 2, 3, half)
    total_qkv = total_qkv.transpose(0, 2, 1, 3).reshape(shard, 3 * width)

    shares = [
        lax.psum_scatter(grad, ("chip", "core"), scatter_dimension=0, tiled=True)
        for grad in (grad_wout, grad_in, grad_down)
    ]
    sums = lax.psum(tuple(shares), seq_axes)
    sums = [value.astype(jnp.float32) for value in sums]

    gain_sums = jnp.stack([grad_first_gain, grad_second_gain])
    gain_sums = gain_sums + core_swap(gain_sums)
    gain_sums = full_sum(full_sum(gain_sums, ("chip",)), seq_axes)
    place = position(("chip", "core"))
    gain_sums = lax.dynamic_slice_in_dim(gain_sums, place * shard, shard, 1)

    return (
        lax.ppermute(layer_out, EVERY, move)[None],
        lax.ppermute(grad_tokens, EVERY, move)[None],
        total_qkv,
        sums[0],
        sums[1],
        sums[2],
        gain_sums[0],
        gain_sums[1],
    )


def solution(mesh):
    devices = mesh.devices
    split = jax.sharding.Mesh(
        devices.reshape(2, devices.shape[0] // 2, devices.shape[1] // 2, 2), EVERY
    )
    seq, fsdp = ("zp", "zi"), ("chip", "core")
    activation, matrix, vector = P(fsdp, seq, None), P(fsdp, None), P(fsdp)
    return jax.shard_map(
        shards,
        mesh=split,
        in_specs=(activation, matrix, matrix, matrix, matrix, vector, vector, vector, activation),
        out_specs=(activation, activation, matrix, matrix, matrix, matrix, vector, vector),
        check_vma=False,
    )
```

```python
import functools
import math

import jax
import jax.numpy as jnp
from jax import lax
from jax.experimental import pallas as pl
from jax.experimental.pallas import tpu as pltpu
from jax.sharding import PartitionSpec as P

HEADS = 12


norm_eps = 1e-05
rope_base = 160000.0
masked_score = -1e30
LANES = 128
EVERY = ("zp", "zi", "chip", "core")
VMEM = 56 << 20


def dot(left, right, left_dim=1, right_dim=0):
    return lax.dot_general(
        left,
        right,
        (((left_dim,), (right_dim,)), ((), ())),
        preferred_element_type=jnp.float32,
    )


def call(kernel, grid, in_specs, out_specs, out_shape, scratch, flops, moved, exps=0, after=()):
    count, extra = len(in_specs), len(after)

    def body(*refs):
        kernel(*refs[:count], *refs[count + extra :])

    made = pl.pallas_call(
        body,
        grid=grid,
        in_specs=list(in_specs) + [pl.BlockSpec(memory_space=pl.ANY)] * extra,
        out_specs=out_specs,
        out_shape=out_shape,
        scratch_shapes=scratch,
        cost_estimate=pl.CostEstimate(flops=flops, bytes_accessed=moved, transcendentals=exps),
        compiler_params=pltpu.CompilerParams(vmem_limit_bytes=VMEM),
    )
    return lambda *args: made(*args, *after)


def shape(dims, dtype):
    return jax.ShapeDtypeStruct(dims, dtype)


def rotary_tables(starts, steps, half_dim):
    lane = jnp.arange(LANES)
    counter = (lane % half_dim).astype(jnp.float32)
    inverse = jnp.exp(counter * (-math.log(rope_base) / half_dim))
    coarse = (starts.astype(jnp.float32)[:, None] * inverse)[:, None, :]
    fine = (jnp.arange(steps).astype(jnp.float32)[:, None] * inverse)[None]
    cosine = jnp.cos(coarse) * jnp.cos(fine) - jnp.sin(coarse) * jnp.sin(fine)
    sine = jnp.sin(coarse) * jnp.cos(fine) + jnp.cos(coarse) * jnp.sin(fine)
    sign = jnp.where(lane % (2 * half_dim) < half_dim, -1.0, 1.0)
    return cosine.reshape(-1, LANES), (sine * sign).reshape(-1, LANES)


def swap_halves(values, head_dim):
    half = head_dim // 2
    lane = lax.broadcasted_iota(jnp.int32, values.shape, 1)
    ahead = pltpu.roll(values, LANES - half, 1)
    behind = pltpu.roll(values, half, 1)
    return jnp.where(lane % head_dim < half, ahead, behind)


def project_kernel(tiles, head_dim, pieces, core, own, other, gain, cosine, sine, *refs):
    step = pl.program_id(0)
    if pieces:
        raw, (h_out, q_out, weight) = refs[:3], refs[4:]
        count, pitch, shard = pieces
        half = raw[0].shape[1]

        @pl.when(step == 0)
        def compact():
            for piece in range(count):
                for third in range(3):
                    weight[
                        piece * shard : (piece + 1) * shard, third * half : (third + 1) * half
                    ] = raw[third][piece * pitch : piece * pitch + shard, :]

        kv_out = refs[3]
    else:
        weight, kv_out = refs
    values = jnp.where(step < tiles, own[...], other[...]).astype(jnp.float32)
    centre = values - jnp.mean(values, -1, keepdims=True)
    spread = jnp.mean(centre * centre, -1, keepdims=True)
    hidden = (centre * lax.rsqrt(spread + norm_eps) * gain[...]).astype(jnp.bfloat16)
    width = weight.shape[1] // 3
    cos, sin = cosine[...], sine[...]
    if pieces:
        h_out[...] = hidden
        joined = dot(hidden, weight[...])
        start = width
    else:
        joined = dot(hidden, weight[:, width:])
        start = 0
    factor = head_dim ** (-0.5) * math.log2(math.e)
    for pair in range(width // LANES):
        at = pair * LANES
        if pieces:
            query = joined[:, at : at + LANES]
            query = query * cos + swap_halves(query, head_dim) * sin
            q_out[:, at : at + LANES] = (query * factor).astype(jnp.bfloat16)
        key = joined[:, start + at : start + at + LANES]
        key = key * cos + swap_halves(key, head_dim) * sin
        kv_out[:, 2 * at : 2 * at + LANES] = key.astype(jnp.bfloat16)
        value = joined[:, start + width + at : start + width + at + LANES]
        kv_out[:, 2 * at + LANES : 2 * at + 2 * LANES] = value.astype(jnp.bfloat16)


def project(core, own, other, gain, weight, cosine, sine, head_dim, pieces=None, after=()):
    rows, depth = own.shape
    block = min(256, rows)
    tiles = rows // block
    half = depth // 2
    by_row = lambda step, core: (step, 0)
    whole = lambda step, core: (0, 0)
    widths = [2 * half] + ([depth, half] if pieces else [])
    outs = [pl.BlockSpec((block, columns), by_row) for columns in widths]
    shapes = [shape((2 * rows, columns), jnp.bfloat16) for columns in widths]
    if pieces:
        weights = [
            pl.BlockSpec((weight.shape[0], half), lambda step, core, third=third: (0, 2 * third + core[0]))
            for third in range(3)
        ]
        outs.append(pl.BlockSpec((depth, 3 * half), whole))
        shapes.append(shape((depth, 3 * half), jnp.bfloat16))
    else:
        weights = [pl.BlockSpec(weight.shape, whole)]
    count = 5 + len(weights)

    def body(core, *refs):
        project_kernel(tiles, head_dim, pieces, core, *refs[:count], *refs[count + len(after) :])

    return pl.pallas_call(
        body,
        grid_spec=pltpu.PrefetchScalarGridSpec(
            num_scalar_prefetch=1,
            grid=(2 * tiles,),
            in_specs=[
                pl.BlockSpec((block, depth), lambda step, core: (jnp.minimum(step, tiles - 1), 0)),
                pl.BlockSpec((block, depth), lambda step, core: (jnp.maximum(step - tiles, 0), 0)),
                pl.BlockSpec((1, depth), whole),
                pl.BlockSpec((block, LANES), by_row),
                pl.BlockSpec((block, LANES), by_row),
            ]
            + weights
            + [pl.BlockSpec(memory_space=pl.ANY)] * len(after),
            out_specs=outs,
        ),
        out_shape=shapes,
        cost_estimate=pl.CostEstimate(
            flops=2 * 2 * rows * depth * 3 * half,
            bytes_accessed=2 * rows * (2 * depth + 3 * half) * 2 + weight.size * 2,
            transcendentals=0,
        ),
        compiler_params=pltpu.CompilerParams(vmem_limit_bytes=VMEM),
    )(core, own, other, gain, cosine, sine, *[weight] * len(weights), *after)


def attend_kernel(head_dim, sources, first, last, *refs):
    refs = list(refs)
    query = refs.pop(0)
    keys = [(refs.pop(0), refs.pop(0)) for _ in range(sources)]
    if not first:
        acc_in, max_in = refs.pop(0), refs.pop(0)
    if last:
        mixed, log_total = refs.pop(0), refs.pop(0)
    else:
        acc_out, max_out = refs.pop(0), refs.pop(0)
    key_of, value_of, bias_of = refs
    span = keys[0][0].shape[0]

    @pl.when(pl.program_id(1) == 0)
    def prepare():
        low = lax.broadcasted_iota(jnp.int32, (span, LANES), 1) < head_dim
        one = jnp.ones((span, LANES), jnp.bfloat16)
        zero = jnp.zeros((span, LANES), jnp.bfloat16)
        for source, (key_value, bias) in enumerate(keys):
            part = pl.ds(source * span, span)
            key, value = key_value[:, :LANES], key_value[:, LANES:]
            key_of[0, part, :] = jnp.where(low, key, zero)
            key_of[1, part, :] = jnp.where(low, zero, key)
            value_of[0, part, :] = jnp.where(low, value, one)
            value_of[1, part, :] = jnp.where(low, one, value)
            bias_of[:, part] = bias[...]

    rows = query.shape[0]
    block = min(512, rows)
    low = lax.broadcasted_iota(jnp.int32, (block, LANES), 1) < head_dim
    for start in range(0, rows, block):
        part = pl.ds(start, block)
        held = query[part, :]
        results, tops = [], []
        for head in range(2):
            score = dot(held, key_of[head], 1, 1) + bias_of[...]
            top = jnp.max(score, 1, keepdims=True)
            if not first:
                before = max_in[part, head * head_dim : head * head_dim + 1]
                top = jnp.maximum(top, before)
            expo = jnp.exp2(score - top).astype(jnp.bfloat16)
            result = dot(expo, value_of[head])
            if not first:
                kept = acc_in[part, head * LANES : (head + 1) * LANES]
                result = result + kept * jnp.exp2(before - top)
            results.append(result)
            tops.append(top)
        top = jnp.where(low, tops[0], tops[1])
        if last:
            total = jnp.where(
                low, pltpu.roll(results[0], head_dim, 1), pltpu.roll(results[1], head_dim, 1)
            )
            mixed[part, :] = (jnp.where(low, results[0], results[1]) / total).astype(mixed.dtype)
            log_total[part, :] = top + jnp.log2(total)
        else:
            acc_out[part, :LANES] = results[0]
            acc_out[part, LANES:] = results[1]
            max_out[part, :] = top


def attend(query, keys, state=None, last=True, head_dim=64, after=()):
    rows, width = query.shape
    span = keys[0][0].shape[0]
    pairs = width // LANES
    block = rows
    narrow = pl.BlockSpec((block, LANES), lambda pair, step: (step, pair))
    wide = pl.BlockSpec((block, 2 * LANES), lambda pair, step: (step, pair))
    in_specs = [narrow]
    args = [query]
    for key_value, bias in keys:
        in_specs += [
            pl.BlockSpec((span, 2 * LANES), lambda pair, step: (0, pair)),
            pl.BlockSpec((1, span), lambda pair, step: (0, 0)),
        ]
        args += [key_value, bias]
    if state is not None:
        in_specs += [wide, narrow]
        args += list(state)
    if last:
        out_specs = [narrow, narrow]
        out_shape = [shape((rows, width), jnp.bfloat16), shape((rows, width), jnp.float32)]
    else:
        out_specs = [wide, narrow]
        out_shape = [shape((rows, 2 * width), jnp.float32), shape((rows, width), jnp.float32)]
    count = span * len(keys)
    return call(
        functools.partial(attend_kernel, head_dim, len(keys), state is None, last),
        (pairs, rows // block),
        in_specs,
        out_specs,
        out_shape,
        [
            pltpu.VMEM((2, count, LANES), jnp.bfloat16),
            pltpu.VMEM((2, count, LANES), jnp.bfloat16),
            pltpu.VMEM((1, count), jnp.float32),
        ],
        pairs * 2 * 2 * 2 * rows * count * 256,
        pairs * (rows * LANES * 8 + count * 512),
        pairs * 2 * rows * count,
        after,
    )(*args)


def revisit_kernel(
    head_dim, key_value, bias, query, mixed, near_grad, far_grad, log_total,
    dq_out, dkv_out, grad_key, grad_value, key_of, value_of,
):
    span = key_value.shape[0]
    step = pl.program_id(1)

    @pl.when(step == 0)
    def prepare():
        low = lax.broadcasted_iota(jnp.int32, (span, LANES), 1) < head_dim
        zero = jnp.zeros((span, LANES), jnp.bfloat16)
        key, value = key_value[:, :LANES], key_value[:, LANES:]
        key_of[0] = jnp.where(low, key, zero)
        key_of[1] = jnp.where(low, zero, key)
        value_of[0] = jnp.where(low, value, zero)
        value_of[1] = jnp.where(low, zero, value)
        grad_key[...] = jnp.zeros_like(grad_key)
        grad_value[...] = jnp.zeros_like(grad_value)

    rows = query.shape[0]
    block = min(256, rows // 2)
    for start in range(0, rows, block):
        part = pl.ds(start, block)
        held = query[part, :]
        if start < rows // 2:
            back = near_grad[part, :]
        else:
            back = far_grad[pl.ds(start - rows // 2, block), :]
        held_t, back_t = held.T, back.T
        product = back.astype(jnp.float32) * mixed[part, :].astype(jnp.float32)
        grad_query = None
        for head in range(2):
            lanes = slice(head * head_dim, (head + 1) * head_dim)
            weighted = jnp.sum(product[:, lanes], 1, keepdims=True)
            log_block = log_total[part, head * head_dim : head * head_dim + 1]
            prob = jnp.exp2(dot(held, key_of[head], 1, 1) + bias[...] - log_block)
            grad_prob = dot(back, value_of[head], 1, 1)
            grad_score = (prob * (grad_prob - weighted)).astype(jnp.bfloat16)
            grad_value[lanes, :] += dot(back_t[lanes], prob.astype(jnp.bfloat16))
            grad_key[lanes, :] += dot(held_t[lanes], grad_score)
            term = dot(grad_score, key_of[head])
            grad_query = term if grad_query is None else grad_query + term
        dq_out[part, :] = grad_query * head_dim ** (-0.5)

    @pl.when(step == pl.num_programs(1) - 1)
    def finish():
        dkv_out[:, :LANES] = (grad_key[...].T * math.log(2.0)).astype(dkv_out.dtype)
        dkv_out[:, LANES:] = grad_value[...].T.astype(dkv_out.dtype)


def revisit(
    query, first, pairs, key_value, bias, mixed, near_grad, far_grad, log_total, head_dim=64, after=()
):
    rows = query.shape[0]
    span = key_value.shape[0]
    of_all = pl.BlockSpec((rows, LANES), lambda pair, step: (0, first + pair))
    half_of_all = pl.BlockSpec((rows // 2, LANES), lambda pair, step: (0, first + pair))
    narrow = pl.BlockSpec((rows, LANES), lambda pair, step: (0, pair))
    return call(
        functools.partial(revisit_kernel, head_dim),
        (pairs, 1),
        [
            pl.BlockSpec((span, 2 * LANES), lambda pair, step: (0, first + pair)),
            pl.BlockSpec((1, span), lambda pair, step: (0, 0)),
            of_all,
            of_all,
            half_of_all,
            half_of_all,
            of_all,
        ],
        [narrow, pl.BlockSpec((span, 2 * LANES), lambda pair, step: (0, pair))],
        [
            shape((rows, pairs * LANES), jnp.float32),
            shape((span, pairs * 2 * LANES), jnp.bfloat16),
        ],
        [
            pltpu.VMEM((LANES, span), jnp.float32),
            pltpu.VMEM((LANES, span), jnp.float32),
            pltpu.VMEM((2, span, LANES), jnp.bfloat16),
            pltpu.VMEM((2, span, LANES), jnp.bfloat16),
        ],
        pairs * 5 * 2 * 2 * rows * span * 200,
        pairs * (rows * LANES * 14 + span * 1024),
        pairs * 2 * rows * span,
        after,
    )(key_value, bias, query, mixed, near_grad, far_grad, log_total)


def feed_kernel(
    core, tokens, mine, theirs, m_out, m_in, m_down, gain, cotangent,
    mixed_out, layer_out, hidden_out, act_out, gate_up_out, resid_out, attn_out, kept_out, given_out,
    gain_out,
):
    width_ff = m_down.shape[0]
    half = theirs.shape[1]
    first_core = core[0] == 0
    near, far = mine[...], theirs[...]
    left = jnp.where(first_core, near, far)
    right = jnp.where(first_core, far, near)
    mixed_out[:, :half] = left
    mixed_out[:, half:] = right
    resid = tokens[...].astype(jnp.float32) + dot(mixed_out[...], m_out[...])
    centre = resid - jnp.mean(resid, -1, keepdims=True)
    inverse = lax.rsqrt(jnp.mean(centre * centre, -1, keepdims=True) + norm_eps)
    unit = centre * inverse
    hidden = (unit * gain[...]).astype(jnp.bfloat16)
    hidden_out[...] = hidden
    gate_up = dot(hidden, m_in[...])
    gate, upper = gate_up[:, :width_ff], gate_up[:, width_ff:]
    phi = 0.5 * (1.0 + lax.erf(gate * math.sqrt(0.5)))
    gelu = gate * phi
    slope = phi + gate * (jnp.exp(-0.5 * gate * gate) * (1.0 / math.sqrt(2.0 * math.pi)))
    act = (gelu * upper).astype(jnp.bfloat16)
    act_out[...] = act
    layer_out[...] = (resid + dot(act, m_down[...])).astype(layer_out.dtype)
    back = cotangent[...]
    grad_act = dot(back, m_down[...], 1, 1)
    gate_up_out[:, :width_ff] = (grad_act * upper * slope).astype(jnp.bfloat16)
    gate_up_out[:, width_ff:] = (grad_act * gelu).astype(jnp.bfloat16)
    grad_hidden = dot(gate_up_out[...], m_in[...], 1, 1)
    share = jnp.sum(grad_hidden * unit, 0, keepdims=True)
    step = pl.program_id(0)

    @pl.when(step == 0)
    def begin():
        gain_out[...] = share

    @pl.when(step > 0)
    def add():
        gain_out[...] += share

    grad_unit = grad_hidden * gain[...]
    grad_resid = back.astype(jnp.float32) + inverse * (
        grad_unit
        - jnp.mean(grad_unit, -1, keepdims=True)
        - unit * jnp.mean(grad_unit * unit, -1, keepdims=True)
    )
    resid_out[...] = grad_resid
    grad_attn = grad_resid.astype(jnp.bfloat16)
    attn_out[...] = grad_attn
    grad_mixed = dot(grad_attn, m_out[...], 1, 1).astype(jnp.bfloat16)
    left, right = grad_mixed[:, :half], grad_mixed[:, half:]
    kept_out[...] = jnp.where(first_core, left, right)
    given_out[...] = jnp.where(first_core, right, left)


def feed(core, tokens, mine, theirs, m_out, m_in, m_down, gain, cotangent):
    rows, width = tokens.shape
    half = width // 2
    block = min(256, rows)
    by_row = lambda step, core: (step, 0)
    whole = lambda step, core: (0, 0)
    row = lambda columns: pl.BlockSpec((block, columns), by_row)
    fixed = lambda array: pl.BlockSpec(array.shape, whole, pipeline_mode=pl.Buffered(1))
    columns = [
        (width, jnp.bfloat16),
        (width, jnp.bfloat16),
        (width, jnp.bfloat16),
        (m_down.shape[0], jnp.bfloat16),
        (m_in.shape[1], jnp.bfloat16),
        (width, jnp.float32),
        (width, jnp.bfloat16),
        (half, jnp.bfloat16),
        (half, jnp.bfloat16),
    ]
    return pl.pallas_call(
        feed_kernel,
        grid_spec=pltpu.PrefetchScalarGridSpec(
            num_scalar_prefetch=1,
            grid=(rows // block,),
            in_specs=[
                row(width),
                row(half),
                row(half),
                fixed(m_out),
                fixed(m_in),
                fixed(m_down),
                pl.BlockSpec((1, width), whole),
                row(width),
            ],
            out_specs=[row(count) for count, _ in columns] + [pl.BlockSpec((1, width), whole)],
        ),
        out_shape=[shape((rows, count), dtype) for count, dtype in columns]
        + [shape((1, width), jnp.float32)],
        cost_estimate=pl.CostEstimate(
            flops=4 * rows * (m_out.size + m_in.size + m_down.size),
            bytes_accessed=2 * (m_out.size + m_in.size + m_down.size) + rows * width * 30,
            transcendentals=2 * rows * m_down.shape[0],
        ),
        compiler_params=pltpu.CompilerParams(vmem_limit_bytes=VMEM),
    )(core, tokens, mine, theirs, m_out, m_in, m_down, gain, cotangent)


def weigh_kernel(shard, shard_down, mixed, attn, hidden, gate_up, act, cotangent, out):
    step = pl.program_id(0)
    width = mixed.shape[1]
    parts = out.shape[0]

    def spread(product, at, rows):
        product = product.astype(out.dtype)
        for part in range(parts):
            out[part, at : at + rows, :] = product[part * rows : (part + 1) * rows]

    for third in range(3):

        @pl.when(step == third)
        def gate(third=third):
            spread(dot(hidden[...], gate_up[...], 0, 0), third * shard, shard)

    @pl.when(step == 3)
    def project_out():
        spread(dot(mixed[...], attn[...], 0, 0), 3 * shard, shard)

    @pl.when(step == 4)
    def down():
        spread(dot(act[...], cotangent[...], 0, 0), 4 * shard, shard_down)
        used = 4 * shard + shard_down
        if used < out.shape[1]:
            out[:, used:, :] = jnp.zeros((parts, out.shape[1] - used, width), out.dtype)


def weigh(shard, shard_down, parts, mixed, attn, hidden, gate_up, act, cotangent):
    rows, width = mixed.shape
    whole = lambda step: (0, 0)
    fixed = lambda array: pl.BlockSpec(array.shape, whole)
    deep = 32 * -(-(4 * shard + shard_down) // 32)
    return call(
        functools.partial(weigh_kernel, shard, shard_down),
        (5,),
        [
            fixed(mixed),
            fixed(attn),
            fixed(hidden),
            pl.BlockSpec((rows, width), lambda step: (0, jnp.minimum(step, 2))),
            fixed(act),
            fixed(cotangent),
        ],
        pl.BlockSpec((parts, deep, width), lambda step: (0, 0, 0)),
        shape((parts, deep, width), jnp.bfloat16),
        [],
        2 * rows * parts * deep * width,
        2 * rows * width * 8 + parts * deep * width * 2,
    )(mixed, attn, hidden, gate_up, act, cotangent)


def unpack_kernel(shard, shard_down, place, *refs):
    parts, (out, gate, down, total) = refs[:4], refs[4:]
    rows, width = parts[0].shape
    for distance in range(4):
        at = pl.multiple_of((place[0] ^ distance) * rows, 8)
        total[pl.ds(at, rows), :] = parts[distance][...].astype(jnp.float32)
    for third in range(3):
        gate[:, third * width : (third + 1) * width] = total[third * shard : (third + 1) * shard, :]
    out[...] = total[3 * shard : 4 * shard, :]
    down[...] = total[4 * shard : 4 * shard + shard_down, :]


def unpack(place, shard, shard_down, parts):
    rows, width = parts[0].shape
    whole = lambda step, place: (0, 0)
    sizes = [(shard, width), (shard, 3 * width), (shard_down, width)]
    return pl.pallas_call(
        functools.partial(unpack_kernel, shard, shard_down),
        grid_spec=pltpu.PrefetchScalarGridSpec(
            num_scalar_prefetch=1,
            grid=(1,),
            in_specs=[pl.BlockSpec((rows, width), whole)] * 4,
            out_specs=[pl.BlockSpec(size, whole) for size in sizes],
            scratch_shapes=[pltpu.VMEM((4 * rows, width), jnp.float32)],
        ),
        out_shape=[shape(size, jnp.float32) for size in sizes],
        cost_estimate=pl.CostEstimate(
            flops=rows * width, bytes_accessed=24 * rows * width, transcendentals=0
        ),
        compiler_params=pltpu.CompilerParams(vmem_limit_bytes=VMEM),
    )(place, *parts)


def gradients(groups, refs, cos, sin, head_dim, put):
    sources = {}
    for (kind, first, pairs), ref in zip(groups, refs):
        for pair in range(pairs):
            sources.setdefault((kind, first + pair), []).append((ref, pair))

    def total(kind, pair, lanes):
        return sum(
            ref[:, place * lanes : (place + 1) * lanes].astype(jnp.float32)
            for ref, place in sources[kind, pair]
        )

    for pair in sorted({pair for _, pair in sources}):
        query = total("query", pair, LANES)
        query = query * cos - swap_halves(query, head_dim) * sin
        put(0, pair, query.astype(jnp.bfloat16))
        both = total("keys", pair, 2 * LANES)
        key, value = both[:, :LANES], both[:, LANES:]
        key = key * cos - swap_halves(key, head_dim) * sin
        put(1, pair, key.astype(jnp.bfloat16))
        put(2, pair, value.astype(jnp.bfloat16))


def group_kinds(groups):
    lanes = {"query": LANES, "keys": 2 * LANES}
    return [(kind, first, array.shape[1] // lanes[kind]) for kind, first, array in groups]


def unproject_kernel(head_dim, groups, weight, cosine, sine, *refs):
    dh_out, joined = refs[-2:]
    width = weight.shape[1] // 3

    def put(kind, pair, values):
        at = kind * width + pair * LANES
        joined[:, at : at + LANES] = values

    gradients(groups, refs[:-2], cosine[...], sine[...], head_dim, put)
    dh_out[...] = dot(joined[...], weight[...], 1, 1).astype(dh_out.dtype)


def unproject(part, weight, cosine, sine, groups, head_dim, after=()):
    rows = cosine.shape[0] // 2
    depth, wide = weight.shape
    block = min(256, rows)
    base = part * (rows // block)
    shifted = lambda columns: pl.BlockSpec((block, columns), lambda step: (base + step, 0))
    return call(
        functools.partial(unproject_kernel, head_dim, group_kinds(groups)),
        (rows // block,),
        [pl.BlockSpec(weight.shape, lambda step: (0, 0)), shifted(LANES), shifted(LANES)]
        + [shifted(array.shape[1]) for _, _, array in groups],
        pl.BlockSpec((block, depth), lambda step: (step, 0)),
        shape((rows, depth), jnp.bfloat16),
        [pltpu.VMEM((block, wide), jnp.bfloat16)],
        2 * rows * weight.size,
        rows * (depth * 4 + wide * 8) + weight.size * 2,
        after=after,
    )(weight, cosine, sine, *[array for _, _, array in groups])


def outer_kernel(chips, head_dim, groups, first, place, hidden, cosine, sine, *refs):
    count = len(groups)
    outs, joined, total = refs[count : count + chips], refs[-2], refs[-1]
    width = joined.shape[1] // 3
    step = pl.program_id(0)

    def put(kind, pair, values):
        at = kind * width + (pair - first) * LANES
        joined[:, at : at + LANES] = values

    gradients(groups, refs[:count], cosine[...], sine[...], head_dim, put)
    share = dot(hidden[...], joined[...], 0, 0)

    @pl.when(step == 0)
    def begin():
        total[...] = share

    @pl.when(step > 0)
    def add():
        total[...] += share

    @pl.when(step == pl.num_programs(0) - 1)
    def finish():
        rows = total.shape[0] // chips
        for distance in range(chips):
            at = pl.multiple_of((place[0] ^ distance) * rows, 16)
            outs[distance][...] = total[pl.ds(at, rows), :].astype(outs[distance].dtype)


def outer(place, chips, hidden, cosine, sine, groups, head_dim, after=()):
    rows, depth = hidden.shape
    kinds = group_kinds(groups)
    found = sorted({first + pair for _, first, pairs in kinds for pair in range(pairs)})
    wide = 3 * LANES * len(found)
    block = min(512, rows)
    part = depth // chips
    row = lambda columns: pl.BlockSpec((block, columns), lambda step, place: (step, 0))
    count = 3 + len(groups)

    def body(place, *refs):
        outer_kernel(
            chips, head_dim, kinds, found[0], place, *refs[:count], *refs[count + len(after) :]
        )

    return pl.pallas_call(
        body,
        grid_spec=pltpu.PrefetchScalarGridSpec(
            num_scalar_prefetch=1,
            grid=(rows // block,),
            in_specs=[row(depth), row(LANES), row(LANES)]
            + [row(array.shape[1]) for _, _, array in groups]
            + [pl.BlockSpec(memory_space=pl.ANY)] * len(after),
            out_specs=[pl.BlockSpec((part, wide), lambda step, place: (0, 0))] * chips,
            scratch_shapes=[
                pltpu.VMEM((block, wide), jnp.bfloat16),
                pltpu.VMEM((depth, wide), jnp.float32),
            ],
        ),
        out_shape=[shape((part, wide), jnp.bfloat16)] * chips,
        cost_estimate=pl.CostEstimate(
            flops=2 * rows * depth * wide,
            bytes_accessed=2 * rows * (depth + 4 * wide) + 2 * depth * wide,
            transcendentals=0,
        ),
        compiler_params=pltpu.CompilerParams(vmem_limit_bytes=VMEM),
    )(place, hidden, cosine, sine, *[array for _, _, array in groups], *after)


def finish_kernel(tokens, near, far, gain, grad_resid, out, gain_out):
    values = tokens[...].astype(jnp.float32)
    centre = values - jnp.mean(values, -1, keepdims=True)
    inverse = lax.rsqrt(jnp.mean(centre * centre, -1, keepdims=True) + norm_eps)
    unit = centre * inverse
    grad_hidden = near[...].astype(jnp.float32) + far[...].astype(jnp.float32)
    share = jnp.sum(grad_hidden * unit, 0, keepdims=True)
    step = pl.program_id(0)

    @pl.when(step == 0)
    def begin():
        gain_out[...] = share

    @pl.when(step > 0)
    def add():
        gain_out[...] += share

    grad_unit = grad_hidden * gain[...]
    grad_norm = inverse * (
        grad_unit
        - jnp.mean(grad_unit, -1, keepdims=True)
        - unit * jnp.mean(grad_unit * unit, -1, keepdims=True)
    )
    out[...] = (grad_resid[...] + grad_norm).astype(out.dtype)


def finish(tokens, near, far, gain, grad_resid):
    rows, width = tokens.shape
    block = min(256, rows)
    row = pl.BlockSpec((block, width), lambda step: (step, 0))
    one = pl.BlockSpec((1, width), lambda step: (0, 0))
    return call(
        finish_kernel,
        (rows // block,),
        [row, row, row, one, row],
        [row, one],
        [shape((rows, width), jnp.bfloat16), shape((1, width), jnp.float32)],
        [],
        rows * width * 20,
        rows * width * 12,
    )(tokens, near, far, gain, grad_resid)


EXTRA = 16


def gain_rows(gains, wide):
    rows, width = gains.shape
    blank = jnp.zeros((rows, wide - width), jnp.float32)
    below = jnp.zeros((EXTRA - rows, wide), jnp.float32)
    return jnp.concatenate([jnp.concatenate([gains, blank], 1), below], 0)


def fold_kernel(chips, place, *refs):
    parts, (first, second), outs, total = refs[:chips], refs[chips : chips + 2], refs[-5:-1], refs[-1]
    total[...] = sum(ref[...].astype(jnp.float32) for ref in parts)
    rows, wide = total.shape[0] // 4, total.shape[1]
    extra = gain_rows(jnp.concatenate([first[...], second[...]], 0), wide)
    for distance in range(4):
        at = pl.multiple_of((place[0] ^ distance) * rows, 8)
        outs[distance][:rows, :] = total[pl.ds(at, rows), :].astype(outs[distance].dtype)
        outs[distance][rows:, :] = extra.astype(outs[distance].dtype)


def fold(place, parts, first, second):
    rows, wide = parts[0].shape
    whole = lambda step, place: (0, 0)
    arrays = [*parts, first, second]
    types = [jnp.float32] + [jnp.bfloat16] * 3
    return pl.pallas_call(
        functools.partial(fold_kernel, len(parts)),
        grid_spec=pltpu.PrefetchScalarGridSpec(
            num_scalar_prefetch=1,
            grid=(1,),
            in_specs=[pl.BlockSpec(array.shape, whole) for array in arrays],
            out_specs=[pl.BlockSpec((rows // 4 + EXTRA, wide), whole)] * 4,
            scratch_shapes=[pltpu.VMEM((rows, wide), jnp.float32)],
        ),
        out_shape=[shape((rows // 4 + EXTRA, wide), dtype) for dtype in types],
        cost_estimate=pl.CostEstimate(
            flops=8 * rows * wide, bytes_accessed=10 * rows * wide, transcendentals=0
        ),
        compiler_params=pltpu.CompilerParams(vmem_limit_bytes=VMEM),
    )(place, *arrays)


def add_kernel(extra, *refs):
    parts, outs = refs[:4], refs[4:]
    total = sum(ref[...].astype(jnp.float32) for ref in parts)
    rows = total.shape[0] - extra
    outs[0][...] = total[:rows].astype(jnp.bfloat16)
    if extra:
        outs[1][...] = total[rows:]


def add(arrays, extra=0, after=()):
    rows, wide = arrays[0].shape
    whole = lambda step: (0, 0)
    sizes = [(rows - extra, wide, jnp.bfloat16)] + ([(extra, wide, jnp.float32)] if extra else [])
    return call(
        functools.partial(add_kernel, extra),
        (1,),
        [pl.BlockSpec((rows, wide), whole)] * 4,
        [pl.BlockSpec((count, wide), whole) for count, _, _ in sizes],
        [shape((count, wide), dtype) for count, _, dtype in sizes],
        [],
        4 * rows * wide,
        10 * rows * wide,
        after=after,
    )(*arrays)


def order_kernel(chips, scalars, *refs):
    parts, gains, (kept, given, gain_out, total) = refs[:4], refs[4 : 4 + chips], refs[4 + chips :]
    rows = parts[0].shape[0]
    for distance in range(4):
        at = pl.multiple_of((scalars[0] ^ distance) * rows, 8)
        total[pl.ds(at, rows), :] = parts[distance][...].astype(jnp.float32)
    half = kept.shape[0]
    first_core = scalars[1] == 0
    upper, lower = total[:half, :], total[half:, :]
    kept[...] = jnp.where(first_core, upper, lower)
    given[:half, :] = jnp.where(first_core, lower, upper).astype(jnp.bfloat16)
    share = sum(ref[...] for ref in gains)
    given[half:, :] = share.astype(jnp.bfloat16)
    gain_out[...] = share


def order(scalars, parts, gains):
    rows, wide = parts[0].shape
    whole = lambda step, scalars: (0, 0)
    sizes = [
        (2 * rows, jnp.float32),
        (2 * rows + EXTRA, jnp.bfloat16),
        (EXTRA, jnp.float32),
    ]
    return pl.pallas_call(
        functools.partial(order_kernel, len(gains)),
        grid_spec=pltpu.PrefetchScalarGridSpec(
            num_scalar_prefetch=1,
            grid=(1,),
            in_specs=[pl.BlockSpec((rows, wide), whole)] * 4
            + [pl.BlockSpec((EXTRA, wide), whole)] * len(gains),
            out_specs=[pl.BlockSpec((count, wide), whole) for count, _ in sizes],
            scratch_shapes=[pltpu.VMEM((4 * rows, wide), jnp.float32)],
        ),
        out_shape=[shape((count, wide), dtype) for count, dtype in sizes],
        cost_estimate=pl.CostEstimate(
            flops=rows * wide, bytes_accessed=24 * rows * wide, transcendentals=0
        ),
        compiler_params=pltpu.CompilerParams(vmem_limit_bytes=VMEM),
    )(scalars, *parts, *gains)


def weave_kernel(scalars, kept, taken, gains, out, gain_out):
    first_core = scalars[0] == 0
    rows = kept.shape[0]
    mine, theirs = kept[...], taken[:rows, :].astype(jnp.float32)
    half = mine.shape[1] // 3
    for third in range(3):
        part = slice(third * half, (third + 1) * half)
        at = 2 * third * half
        out[:, at : at + half] = jnp.where(first_core, mine[:, part], theirs[:, part])
        out[:, at + half : at + 2 * half] = jnp.where(first_core, theirs[:, part], mine[:, part])
    total = (gains[...] + taken[rows:, :].astype(jnp.float32))[:8]
    found = jnp.zeros((8, rows), jnp.float32)
    for device in range(2 * half // rows):
        found = jnp.where(scalars[1] == device, total[:, device * rows : (device + 1) * rows], found)
    gain_out[...] = found


def weave(scalars, kept, taken, gains):
    rows, wide = kept.shape
    arrays = (kept, taken, gains)
    whole = lambda step, scalars: (0, 0)
    return pl.pallas_call(
        weave_kernel,
        grid_spec=pltpu.PrefetchScalarGridSpec(
            num_scalar_prefetch=1,
            grid=(1,),
            in_specs=[pl.BlockSpec(array.shape, whole) for array in arrays],
            out_specs=[pl.BlockSpec((rows, 2 * wide), whole), pl.BlockSpec((8, rows), whole)],
        ),
        out_shape=[shape((rows, 2 * wide), jnp.float32), shape((8, rows), jnp.float32)],
        cost_estimate=pl.CostEstimate(
            flops=rows * wide, bytes_accessed=14 * rows * wide, transcendentals=0
        ),
        compiler_params=pltpu.CompilerParams(vmem_limit_bytes=VMEM),
    )(scalars, *arrays)


def position(axes):
    place = 0
    for axis in axes:
        place = place * lax.axis_size(axis) + lax.axis_index(axis)
    return place


def others(axes):
    count = math.prod(lax.axis_size(axis) for axis in axes)
    return count, [
        [(source, source ^ step) for source in range(count)] for step in range(1, count)
    ]


def exchange(block, axes):
    _, steps = others(axes)
    return [block] + [lax.ppermute(block, axes, pairs) for pairs in steps]


def placed(parts, axes):
    place = position(axes)
    rows = parts[0].shape[0]
    whole = jnp.zeros((len(parts) * rows,) + parts[0].shape[1:], parts[0].dtype)
    for step, part in enumerate(parts):
        whole = lax.dynamic_update_slice_in_dim(whole, part, (place ^ step) * rows, 0)
    return whole


def gather(block, axes):
    if others(axes)[0] > 4:
        return lax.all_gather(block, axes, axis=0, tiled=True)
    return placed(exchange(block, axes), axes)


def receive(parts, axes):
    _, steps = others(axes)
    return [parts[0]] + [
        lax.ppermute(part, axes, pairs) for part, pairs in zip(parts[1:], steps)
    ]


def sum_blocks(parts, axes):
    _, steps = others(axes)
    total = parts[0].astype(jnp.float32)
    for part, pairs in zip(parts[1:], steps):
        total = total + lax.ppermute(part, axes, pairs).astype(jnp.float32)
    return total


def scatter_sum(whole, axes):
    count, _ = others(axes)
    if count > 4:
        return lax.psum_scatter(whole, axes, scatter_dimension=0, tiled=True).astype(jnp.float32)
    place = position(axes)
    rows = whole.shape[0] // count
    return sum_blocks(
        [
            lax.dynamic_slice_in_dim(whole, (place ^ step) * rows, rows, 0)
            for step in range(count)
        ],
        axes,
    )


def full_sum(values, axes):
    count, steps = others(axes)
    if count > 4:
        return lax.psum(values, axes)
    return values + sum(lax.ppermute(values, axes, pairs) for pairs in steps)


def core_swap(block):
    return lax.ppermute(block, "core", [(0, 1), (1, 0)])


def later(arrays, first):
    return lax.optimization_barrier((arrays, first))[0]


def shards(tokens, w_qkv, w_out, w_in, w_down, gain_attn, gain_mlp, lengths, cotangent):
    rows, width = tokens.shape[1:]
    head_dim = width // HEADS
    half = width // 2
    pairs = half // LANES
    chips = lax.axis_size("chip")
    core, inner = lax.axis_index("core"), lax.axis_index("zi")
    first_core = core == 0
    seq_axes, fsdp_axes = ("zp", "zi"), ("chip", "core")
    low = jnp.bfloat16
    few = chips <= 4

    places = [
        (zp, zi, chip, c)
        for zp in range(2)
        for zi in range(2)
        for chip in range(chips)
        for c in range(2)
    ]
    number = {place: index for index, place in enumerate(places)}
    moves = [
        (number[(zp, zi, chip, c)], number[(c, zi, chip, zp)])
        for zp, zi, chip, c in places
        if zp != c
    ]
    stays = lax.axis_index("zp") == core

    def move(array):
        return jnp.where(stays, array, lax.ppermute(array, EVERY, moves))

    swap_chips = [(0, 1), (1, 0)]
    own = move(tokens[0])
    other = core_swap(own)
    far_own = lax.ppermute(own, "zi", swap_chips)
    far_other = core_swap(far_own)

    shard = w_qkv.shape[0]
    pitch = -(-(shard + 1) // 16) * 16
    devices = 2 * chips
    exact = jnp.stack([lengths[0] // 64, lengths[0] % 64]).astype(low)
    filler = jnp.zeros((3 * width - 2 * shard - 2,), low)
    gains = jnp.concatenate([gain_attn, gain_mlp, exact, filler])
    block = jnp.concatenate([w_qkv, jnp.broadcast_to(gains[None], (pitch - shard, 3 * width))], 0)
    raw = lax.all_gather(block, fsdp_axes, axis=0, tiled=True)
    all_gains = raw.reshape(devices, pitch, 3 * width)[:, shard, : 2 * shard + 2].astype(jnp.float32)
    first_gain = all_gains[:, :shard].reshape(1, width)
    second_gain = all_gains[:, shard : 2 * shard].reshape(1, width)
    sequence = 2 * lax.axis_index("chip") + lax.axis_index("zp")
    exact = lax.dynamic_slice_in_dim(all_gains[:, 2 * shard :], sequence, 1, 0)[0]
    length = (exact[0] * 64 + exact[1]).astype(jnp.int32)
    pieces = (devices, pitch, shard)
    if shard % 16:
        raw = raw.reshape(devices, pitch, 3 * width)[:, :shard].reshape(width, 3 * width)
        pieces = (1, width, width)

    grad_out = move(later(cotangent[0], far_own))
    w_out, w_in, w_down = later((w_out, w_in, w_down), own)
    m_out = lax.all_gather(w_out, fsdp_axes, axis=0, tiled=True)
    m_in = lax.all_gather(w_in, fsdp_axes, axis=0, tiled=True)
    m_down = lax.all_gather(w_down, fsdp_axes, axis=0, tiled=True)

    steps = jnp.arange(rows)
    own_at = (2 * core + inner) * rows + steps
    other_at = (2 * (1 - core) + inner) * rows + steps
    here = jnp.concatenate([own_at, other_at])
    there = here + jnp.where(inner == 0, rows, -rows)
    run = 64 if rows % 64 == 0 else rows
    cosine, sine = rotary_tables(here[::run], run, head_dim // 2)
    far_cosine, far_sine = rotary_tables(there[::run], run, head_dim // 2)
    near_bias = jnp.where(here < length, 0.0, masked_score).astype(jnp.float32)[None]
    far_bias = jnp.where(there < length, 0.0, masked_score).astype(jnp.float32)[None]

    near, hidden, query, weight = project(
        core[None], own, other, first_gain, raw, cosine, sine, head_dim, pieces
    )
    state = attend(query, [(near, near_bias)], last=False)
    (far,) = project(
        core[None], far_own, far_other, first_gain, weight, far_cosine, far_sine, head_dim,
        after=(state[1],),
    )
    attended, log_total = attend(query, [(far, far_bias)], state)

    theirs = core_swap(attended[rows:])
    (
        mixed,
        layer_out,
        h_second,
        act,
        grad_gate_up,
        grad_resid,
        grad_attn,
        near_back,
        given_back,
        grad_second_gain,
    ) = feed(core[None], own, attended, theirs, m_out, m_in, m_down, second_gain, grad_out)
    layer_out = move(layer_out)
    far_back = core_swap(given_back)

    shard_down = w_down.shape[0]
    if shard % 16 == 0 and shard_down % 16 == 0:
        packed = weigh(
            shard, shard_down, 2 * chips, mixed, grad_attn, h_second, grad_gate_up, act, grad_out
        )
        packed = lax.psum_scatter(packed, fsdp_axes, scatter_dimension=0, tiled=True)[0]
    else:
        grads = (
            dot(h_second, grad_gate_up, 0, 0).reshape(-1, shard, 3, width).transpose(0, 2, 1, 3),
            dot(mixed, grad_attn, 0, 0).reshape(-1, 1, shard, width),
            dot(act, grad_out, 0, 0).reshape(-1, 1, shard_down, width),
        )
        packed = jnp.concatenate(
            [grad.astype(low).reshape(2 * chips, -1, width) for grad in grads], 1
        )
        packed = lax.psum_scatter(packed, fsdp_axes, scatter_dimension=0, tiled=True)[0]

    def back_through(first, count, key_value, bias, after=()):
        return revisit(
            query, first, count, key_value, bias, attended, near_back, far_back, log_total, after=after
        )

    cuts = [(0, pairs - 1), (pairs - 1, 1)]
    tall = few and shard % 16 == 0 and shard_down % 16 == 0
    along = position(seq_axes)
    most = pairs - 1
    far_most = back_through(0, most, far, far_bias)
    far_rest = back_through(most, 1, far, far_bias, (far_most[1],))
    returned = [lax.ppermute(grads[1], "zi", swap_chips) for grads in (far_most, far_rest)]
    near_most = back_through(0, most, near, near_bias, (far_rest[1], layer_out))
    near_rest = back_through(most, 1, near, near_bias, (near_most[1], packed))
    far_grads, near_grads = (far_most, far_rest), (near_most, near_rest)
    after = ()
    if tall:
        deep = packed.shape[0] // 4
        quarters = [
            lax.dynamic_slice_in_dim(packed, (along ^ distance) * deep, deep, 0)
            for distance in range(4)
        ]
        (packed,) = add(receive(quarters, seq_axes), after=(near_rest[1],))
        after = (packed,)
        sums = unpack(along[None], shard, shard_down, exchange(packed, seq_axes))
    else:
        packed = lax.psum(packed, seq_axes).astype(jnp.float32)
        total_in = jnp.concatenate([packed[at * shard : (at + 1) * shard] for at in range(3)], 1)
        sums = (packed[3 * shard : 4 * shard], total_in, packed[4 * shard :])
    groups = [
        [
            ("query", first, near_grads[cut][0]),
            ("query", first, far_grads[cut][0]),
            ("keys", first, near_grads[cut][1]),
            ("keys", first, returned[cut]),
        ]
        for cut, first in enumerate((0, most))
    ]
    every = groups[0] + groups[1]

    place = lax.axis_index("chip")
    if tall:
        parts = outer(place[None], chips, hidden, cosine, sine, every, head_dim, after)
        after = (parts[0],)
        parts = receive(parts, ("chip",))
    else:
        (parts,) = outer(place[None] * 0, 1, hidden, cosine, sine, every, head_dim)
        after = ()
    other_back = unproject(1, weight, cosine, sine, every, head_dim, after)
    other_hidden = core_swap(other_back)
    own_hidden = unproject(0, weight, cosine, sine, every, head_dim, (other_back,))
    grad_tokens, grad_first_gain = finish(own, own_hidden, other_hidden, first_gain, grad_resid)
    if tall:
        blocks = fold(along[None], parts, grad_first_gain, grad_second_gain)
        grad_tokens = move(grad_tokens)
        mine, gain_sums = add(receive(blocks, seq_axes), EXTRA, (grad_tokens,))
        gain_sums = exchange(gain_sums, ("chip",))
        kept, given, gain_sums = order(
            jnp.stack([along, core]), exchange(mine, seq_axes), gain_sums
        )
        total_qkv, gain_sums = weave(
            jnp.stack([core, position(fsdp_axes)]), kept, core_swap(given), gain_sums
        )
    else:
        grad_tokens = move(grad_tokens)
        total = scatter_sum(parts, ("chip",))
        total = scatter_sum(total.astype(low), seq_axes).astype(low)
        total = gather(total, seq_axes)
        kept = jnp.where(first_core, total[:shard], total[shard:])
        given = jnp.where(first_core, total[shard:], total[:shard])
        taken = core_swap(given)
        total_qkv = jnp.where(
            first_core, jnp.stack([kept, taken], 1), jnp.stack([taken, kept], 1)
        ).reshape(shard, 2, 3, half)
        total_qkv = total_qkv.transpose(0, 2, 1, 3).reshape(shard, 3 * width).astype(jnp.float32)

        gain_sums = jnp.concatenate([grad_first_gain, grad_second_gain], 0)
        gain_sums = gain_sums + core_swap(gain_sums)
        gain_sums = full_sum(full_sum(gain_sums, ("chip",)), seq_axes)
        gain_sums = lax.dynamic_slice_in_dim(gain_sums, position(fsdp_axes) * shard, shard, 1)

    return (
        layer_out[None],
        grad_tokens[None],
        total_qkv,
        *sums,
        gain_sums[0],
        gain_sums[1],
    )


def solution(mesh):
    devices = mesh.devices
    split = jax.sharding.Mesh(
        devices.reshape(2, devices.shape[0] // 2, devices.shape[1] // 2, 2), EVERY
    )
    seq, fsdp = ("zp", "zi"), ("chip", "core")
    activation, matrix, vector = P(fsdp, seq, None), P(fsdp, None), P(fsdp)
    return jax.shard_map(
        shards,
        mesh=split,
        in_specs=(activation, matrix, matrix, matrix, matrix, vector, vector, vector, activation),
        out_specs=(activation, activation, matrix, matrix, matrix, matrix, vector, vector),
        check_vma=False,
    )
```

```python
import functools
import math

import jax
import jax.numpy as jnp
from jax import lax
from jax.experimental import pallas as pl
from jax.experimental.pallas import tpu as pltpu
from jax.sharding import PartitionSpec as P

HEADS = 12


norm_eps = 1e-05
rope_base = 160000.0
masked_score = -1e30
LANES = 128
EVERY = ("zp", "zi", "chip", "core")
VMEM = 56 << 20


def dot(left, right, left_dim=1, right_dim=0):
    return lax.dot_general(
        left,
        right,
        (((left_dim,), (right_dim,)), ((), ())),
        preferred_element_type=jnp.float32,
    )


def call(kernel, grid, in_specs, out_specs, out_shape, scratch, flops, moved, exps=0, after=()):
    count, extra = len(in_specs), len(after)

    def body(*refs):
        kernel(*refs[:count], *refs[count + extra :])

    made = pl.pallas_call(
        body,
        grid=grid,
        in_specs=list(in_specs) + [pl.BlockSpec(memory_space=pl.ANY)] * extra,
        out_specs=out_specs,
        out_shape=out_shape,
        scratch_shapes=scratch,
        cost_estimate=pl.CostEstimate(flops=flops, bytes_accessed=moved, transcendentals=exps),
        compiler_params=pltpu.CompilerParams(vmem_limit_bytes=VMEM),
    )
    return lambda *args: made(*args, *after)


def shape(dims, dtype):
    return jax.ShapeDtypeStruct(dims, dtype)


def rotary_tables(starts, steps, half_dim):
    lane = jnp.arange(LANES)
    counter = (lane % half_dim).astype(jnp.float32)
    inverse = jnp.exp(counter * (-math.log(rope_base) / half_dim))
    coarse = (starts.astype(jnp.float32)[:, None] * inverse)[:, None, :]
    fine = (jnp.arange(steps).astype(jnp.float32)[:, None] * inverse)[None]
    cosine = jnp.cos(coarse) * jnp.cos(fine) - jnp.sin(coarse) * jnp.sin(fine)
    sine = jnp.sin(coarse) * jnp.cos(fine) + jnp.cos(coarse) * jnp.sin(fine)
    sign = jnp.where(lane % (2 * half_dim) < half_dim, -1.0, 1.0)
    return cosine.reshape(-1, LANES), (sine * sign).reshape(-1, LANES)


def swap_halves(values, head_dim):
    half = head_dim // 2
    lane = lax.broadcasted_iota(jnp.int32, values.shape, 1)
    ahead = pltpu.roll(values, LANES - half, 1)
    behind = pltpu.roll(values, half, 1)
    return jnp.where(lane % head_dim < half, ahead, behind)


def project_kernel(tiles, head_dim, pieces, core, own, other, gain, cosine, sine, *refs):
    step = pl.program_id(0)
    if pieces:
        raw, (h_out, q_out, weight) = refs[:3], refs[4:]
        count, pitch, shard = pieces
        half = raw[0].shape[1]

        @pl.when(step == 0)
        def compact():
            for piece in range(count):
                for third in range(3):
                    weight[
                        piece * shard : (piece + 1) * shard, third * half : (third + 1) * half
                    ] = raw[third][piece * pitch : piece * pitch + shard, :]

        kv_out = refs[3]
    else:
        weight, kv_out = refs
    values = jnp.where(step < tiles, own[...], other[...]).astype(jnp.float32)
    centre = values - jnp.mean(values, -1, keepdims=True)
    spread = jnp.mean(centre * centre, -1, keepdims=True)
    hidden = (centre * lax.rsqrt(spread + norm_eps) * gain[...]).astype(jnp.bfloat16)
    width = weight.shape[1] // 3
    cos, sin = cosine[...], sine[...]
    if pieces:
        h_out[...] = hidden
        joined = dot(hidden, weight[...])
        start = width
    else:
        joined = dot(hidden, weight[:, width:])
        start = 0
    factor = head_dim ** (-0.5) * math.log2(math.e)
    for pair in range(width // LANES):
        at = pair * LANES
        if pieces:
            query = joined[:, at : at + LANES]
            query = query * cos + swap_halves(query, head_dim) * sin
            q_out[:, at : at + LANES] = (query * factor).astype(jnp.bfloat16)
        key = joined[:, start + at : start + at + LANES]
        key = key * cos + swap_halves(key, head_dim) * sin
        kv_out[:, 2 * at : 2 * at + LANES] = key.astype(jnp.bfloat16)
        value = joined[:, start + width + at : start + width + at + LANES]
        kv_out[:, 2 * at + LANES : 2 * at + 2 * LANES] = value.astype(jnp.bfloat16)


def project(core, own, other, gain, weight, cosine, sine, head_dim, pieces=None, after=()):
    rows, depth = own.shape
    block = min(256, rows)
    tiles = rows // block
    half = depth // 2
    by_row = lambda step, core: (step, 0)
    whole = lambda step, core: (0, 0)
    widths = [2 * half] + ([depth, half] if pieces else [])
    outs = [pl.BlockSpec((block, columns), by_row) for columns in widths]
    shapes = [shape((2 * rows, columns), jnp.bfloat16) for columns in widths]
    if pieces:
        weights = [
            pl.BlockSpec((weight.shape[0], half), lambda step, core, third=third: (0, 2 * third + core[0]))
            for third in range(3)
        ]
        outs.append(pl.BlockSpec((depth, 3 * half), whole))
        shapes.append(shape((depth, 3 * half), jnp.bfloat16))
    else:
        weights = [pl.BlockSpec(weight.shape, whole)]
    count = 5 + len(weights)

    def body(core, *refs):
        project_kernel(tiles, head_dim, pieces, core, *refs[:count], *refs[count + len(after) :])

    return pl.pallas_call(
        body,
        grid_spec=pltpu.PrefetchScalarGridSpec(
            num_scalar_prefetch=1,
            grid=(2 * tiles,),
            in_specs=[
                pl.BlockSpec((block, depth), lambda step, core: (jnp.minimum(step, tiles - 1), 0)),
                pl.BlockSpec((block, depth), lambda step, core: (jnp.maximum(step - tiles, 0), 0)),
                pl.BlockSpec((1, depth), whole),
                pl.BlockSpec((block, LANES), by_row),
                pl.BlockSpec((block, LANES), by_row),
            ]
            + weights
            + [pl.BlockSpec(memory_space=pl.ANY)] * len(after),
            out_specs=outs,
        ),
        out_shape=shapes,
        cost_estimate=pl.CostEstimate(
            flops=2 * 2 * rows * depth * 3 * half,
            bytes_accessed=2 * rows * (2 * depth + 3 * half) * 2 + weight.size * 2,
            transcendentals=0,
        ),
        compiler_params=pltpu.CompilerParams(vmem_limit_bytes=VMEM),
    )(core, own, other, gain, cosine, sine, *[weight] * len(weights), *after)


def attend_kernel(head_dim, sources, first, last, *refs):
    refs = list(refs)
    query = refs.pop(0)
    keys = [(refs.pop(0), refs.pop(0)) for _ in range(sources)]
    if not first:
        acc_in, max_in = refs.pop(0), refs.pop(0)
    if last:
        mixed, log_total = refs.pop(0), refs.pop(0)
    else:
        acc_out, max_out = refs.pop(0), refs.pop(0)
    key_of, value_of, bias_of = refs
    span = keys[0][0].shape[0]

    @pl.when(pl.program_id(1) == 0)
    def prepare():
        low = lax.broadcasted_iota(jnp.int32, (span, LANES), 1) < head_dim
        one = jnp.ones((span, LANES), jnp.bfloat16)
        zero = jnp.zeros((span, LANES), jnp.bfloat16)
        for source, (key_value, bias) in enumerate(keys):
            part = pl.ds(source * span, span)
            key, value = key_value[:, :LANES], key_value[:, LANES:]
            key_of[0, part, :] = jnp.where(low, key, zero)
            key_of[1, part, :] = jnp.where(low, zero, key)
            value_of[0, part, :] = jnp.where(low, value, one)
            value_of[1, part, :] = jnp.where(low, one, value)
            bias_of[:, part] = bias[...]

    rows = query.shape[0]
    block = min(512, rows)
    low = lax.broadcasted_iota(jnp.int32, (block, LANES), 1) < head_dim
    for start in range(0, rows, block):
        part = pl.ds(start, block)
        held = query[part, :]
        results, tops = [], []
        for head in range(2):
            score = dot(held, key_of[head], 1, 1) + bias_of[...]
            top = jnp.max(score, 1, keepdims=True)
            if not first:
                before = max_in[part, head * head_dim : head * head_dim + 1]
                top = jnp.maximum(top, before)
            expo = jnp.exp2(score - top).astype(jnp.bfloat16)
            result = dot(expo, value_of[head])
            if not first:
                kept = acc_in[part, head * LANES : (head + 1) * LANES]
                result = result + kept * jnp.exp2(before - top)
            results.append(result)
            tops.append(top)
        top = jnp.where(low, tops[0], tops[1])
        if last:
            total = jnp.where(
                low, pltpu.roll(results[0], head_dim, 1), pltpu.roll(results[1], head_dim, 1)
            )
            mixed[part, :] = (jnp.where(low, results[0], results[1]) / total).astype(mixed.dtype)
            log_total[part, :] = top + jnp.log2(total)
        else:
            acc_out[part, :LANES] = results[0]
            acc_out[part, LANES:] = results[1]
            max_out[part, :] = top


def attend(query, keys, state=None, last=True, head_dim=64, after=()):
    rows, width = query.shape
    span = keys[0][0].shape[0]
    pairs = width // LANES
    block = rows
    narrow = pl.BlockSpec((block, LANES), lambda pair, step: (step, pair))
    wide = pl.BlockSpec((block, 2 * LANES), lambda pair, step: (step, pair))
    in_specs = [narrow]
    args = [query]
    for key_value, bias in keys:
        in_specs += [
            pl.BlockSpec((span, 2 * LANES), lambda pair, step: (0, pair)),
            pl.BlockSpec((1, span), lambda pair, step: (0, 0)),
        ]
        args += [key_value, bias]
    if state is not None:
        in_specs += [wide, narrow]
        args += list(state)
    if last:
        out_specs = [narrow, narrow]
        out_shape = [shape((rows, width), jnp.bfloat16), shape((rows, width), jnp.float32)]
    else:
        out_specs = [wide, narrow]
        out_shape = [shape((rows, 2 * width), jnp.float32), shape((rows, width), jnp.float32)]
    count = span * len(keys)
    return call(
        functools.partial(attend_kernel, head_dim, len(keys), state is None, last),
        (pairs, rows // block),
        in_specs,
        out_specs,
        out_shape,
        [
            pltpu.VMEM((2, count, LANES), jnp.bfloat16),
            pltpu.VMEM((2, count, LANES), jnp.bfloat16),
            pltpu.VMEM((1, count), jnp.float32),
        ],
        pairs * 2 * 2 * 2 * rows * count * 256,
        pairs * (rows * LANES * 8 + count * 512),
        pairs * 2 * rows * count,
        after,
    )(*args)


def revisit_kernel(
    head_dim, key_value, bias, query, mixed, near_grad, far_grad, log_total,
    dq_out, dkv_out, grad_key, grad_value, key_of, value_of,
):
    span = key_value.shape[0]
    step = pl.program_id(1)

    @pl.when(step == 0)
    def prepare():
        low = lax.broadcasted_iota(jnp.int32, (span, LANES), 1) < head_dim
        zero = jnp.zeros((span, LANES), jnp.bfloat16)
        key, value = key_value[:, :LANES], key_value[:, LANES:]
        key_of[0] = jnp.where(low, key, zero)
        key_of[1] = jnp.where(low, zero, key)
        value_of[0] = jnp.where(low, value, zero)
        value_of[1] = jnp.where(low, zero, value)
        grad_key[...] = jnp.zeros_like(grad_key)
        grad_value[...] = jnp.zeros_like(grad_value)

    rows = query.shape[0]
    block = min(256, rows // 2)
    for start in range(0, rows, block):
        part = pl.ds(start, block)
        held = query[part, :]
        if start < rows // 2:
            back = near_grad[part, :]
        else:
            back = far_grad[pl.ds(start - rows // 2, block), :]
        held_t, back_t = held.T, back.T
        product = back.astype(jnp.float32) * mixed[part, :].astype(jnp.float32)
        grad_query = None
        for head in range(2):
            lanes = slice(head * head_dim, (head + 1) * head_dim)
            weighted = jnp.sum(product[:, lanes], 1, keepdims=True)
            log_block = log_total[part, head * head_dim : head * head_dim + 1]
            prob = jnp.exp2(dot(held, key_of[head], 1, 1) + bias[...] - log_block)
            grad_prob = dot(back, value_of[head], 1, 1)
            grad_score = (prob * (grad_prob - weighted)).astype(jnp.bfloat16)
            grad_value[lanes, :] += dot(back_t[lanes], prob.astype(jnp.bfloat16))
            grad_key[lanes, :] += dot(held_t[lanes], grad_score)
            term = dot(grad_score, key_of[head])
            grad_query = term if grad_query is None else grad_query + term
        dq_out[part, :] = grad_query * head_dim ** (-0.5)

    @pl.when(step == pl.num_programs(1) - 1)
    def finish():
        dkv_out[:, :LANES] = (grad_key[...].T * math.log(2.0)).astype(dkv_out.dtype)
        dkv_out[:, LANES:] = grad_value[...].T.astype(dkv_out.dtype)


def revisit(
    query, first, pairs, key_value, bias, mixed, near_grad, far_grad, log_total, head_dim=64, after=()
):
    rows = query.shape[0]
    span = key_value.shape[0]
    of_all = pl.BlockSpec((rows, LANES), lambda pair, step: (0, first + pair))
    half_of_all = pl.BlockSpec((rows // 2, LANES), lambda pair, step: (0, first + pair))
    narrow = pl.BlockSpec((rows, LANES), lambda pair, step: (0, pair))
    return call(
        functools.partial(revisit_kernel, head_dim),
        (pairs, 1),
        [
            pl.BlockSpec((span, 2 * LANES), lambda pair, step: (0, first + pair)),
            pl.BlockSpec((1, span), lambda pair, step: (0, 0)),
            of_all,
            of_all,
            half_of_all,
            half_of_all,
            of_all,
        ],
        [narrow, pl.BlockSpec((span, 2 * LANES), lambda pair, step: (0, pair))],
        [
            shape((rows, pairs * LANES), jnp.float32),
            shape((span, pairs * 2 * LANES), jnp.bfloat16),
        ],
        [
            pltpu.VMEM((LANES, span), jnp.float32),
            pltpu.VMEM((LANES, span), jnp.float32),
            pltpu.VMEM((2, span, LANES), jnp.bfloat16),
            pltpu.VMEM((2, span, LANES), jnp.bfloat16),
        ],
        pairs * 5 * 2 * 2 * rows * span * 200,
        pairs * (rows * LANES * 14 + span * 1024),
        pairs * 2 * rows * span,
        after,
    )(key_value, bias, query, mixed, near_grad, far_grad, log_total)


def feed_kernel(
    core, tokens, mine, theirs, m_out, m_in, m_down, gain, cotangent,
    mixed_out, layer_out, hidden_out, act_out, gate_up_out, resid_out, attn_out, kept_out, given_out,
    gain_out,
):
    width_ff = m_down.shape[0]
    half = theirs.shape[1]
    first_core = core[0] == 0
    near, far = mine[...], theirs[...]
    left = jnp.where(first_core, near, far)
    right = jnp.where(first_core, far, near)
    mixed_out[:, :half] = left
    mixed_out[:, half:] = right
    resid = tokens[...].astype(jnp.float32) + dot(mixed_out[...], m_out[...])
    centre = resid - jnp.mean(resid, -1, keepdims=True)
    inverse = lax.rsqrt(jnp.mean(centre * centre, -1, keepdims=True) + norm_eps)
    unit = centre * inverse
    hidden = (unit * gain[...]).astype(jnp.bfloat16)
    hidden_out[...] = hidden
    gate_up = dot(hidden, m_in[...])
    gate, upper = gate_up[:, :width_ff], gate_up[:, width_ff:]
    phi = 0.5 * (1.0 + lax.erf(gate * math.sqrt(0.5)))
    gelu = gate * phi
    slope = phi + gate * (jnp.exp(-0.5 * gate * gate) * (1.0 / math.sqrt(2.0 * math.pi)))
    act = (gelu * upper).astype(jnp.bfloat16)
    act_out[...] = act
    layer_out[...] = (resid + dot(act, m_down[...])).astype(layer_out.dtype)
    back = cotangent[...]
    grad_act = dot(back, m_down[...], 1, 1)
    gate_up_out[:, :width_ff] = (grad_act * upper * slope).astype(jnp.bfloat16)
    gate_up_out[:, width_ff:] = (grad_act * gelu).astype(jnp.bfloat16)
    grad_hidden = dot(gate_up_out[...], m_in[...], 1, 1)
    share = jnp.sum(grad_hidden * unit, 0, keepdims=True)
    step = pl.program_id(0)

    @pl.when(step == 0)
    def begin():
        gain_out[...] = share

    @pl.when(step > 0)
    def add():
        gain_out[...] += share

    grad_unit = grad_hidden * gain[...]
    grad_resid = back.astype(jnp.float32) + inverse * (
        grad_unit
        - jnp.mean(grad_unit, -1, keepdims=True)
        - unit * jnp.mean(grad_unit * unit, -1, keepdims=True)
    )
    resid_out[...] = grad_resid
    grad_attn = grad_resid.astype(jnp.bfloat16)
    attn_out[...] = grad_attn
    grad_mixed = dot(grad_attn, m_out[...], 1, 1).astype(jnp.bfloat16)
    left, right = grad_mixed[:, :half], grad_mixed[:, half:]
    kept_out[...] = jnp.where(first_core, left, right)
    given_out[...] = jnp.where(first_core, right, left)


def feed(core, tokens, mine, theirs, m_out, m_in, m_down, gain, cotangent):
    rows, width = tokens.shape
    half = width // 2
    block = min(256, rows)
    by_row = lambda step, core: (step, 0)
    whole = lambda step, core: (0, 0)
    row = lambda columns: pl.BlockSpec((block, columns), by_row)
    fixed = lambda array: pl.BlockSpec(array.shape, whole, pipeline_mode=pl.Buffered(1))
    columns = [
        (width, jnp.bfloat16),
        (width, jnp.bfloat16),
        (width, jnp.bfloat16),
        (m_down.shape[0], jnp.bfloat16),
        (m_in.shape[1], jnp.bfloat16),
        (width, jnp.float32),
        (width, jnp.bfloat16),
        (half, jnp.bfloat16),
        (half, jnp.bfloat16),
    ]
    return pl.pallas_call(
        feed_kernel,
        grid_spec=pltpu.PrefetchScalarGridSpec(
            num_scalar_prefetch=1,
            grid=(rows // block,),
            in_specs=[
                row(width),
                row(half),
                row(half),
                fixed(m_out),
                fixed(m_in),
                fixed(m_down),
                pl.BlockSpec((1, width), whole),
                row(width),
            ],
            out_specs=[row(count) for count, _ in columns] + [pl.BlockSpec((1, width), whole)],
        ),
        out_shape=[shape((rows, count), dtype) for count, dtype in columns]
        + [shape((1, width), jnp.float32)],
        cost_estimate=pl.CostEstimate(
            flops=4 * rows * (m_out.size + m_in.size + m_down.size),
            bytes_accessed=2 * (m_out.size + m_in.size + m_down.size) + rows * width * 30,
            transcendentals=2 * rows * m_down.shape[0],
        ),
        compiler_params=pltpu.CompilerParams(vmem_limit_bytes=VMEM),
    )(core, tokens, mine, theirs, m_out, m_in, m_down, gain, cotangent)


def weigh_kernel(shard, shard_down, mixed, attn, hidden, gate_up, act, cotangent, out):
    step = pl.program_id(0)
    width = mixed.shape[1]
    parts = out.shape[0]

    def spread(product, at, rows):
        product = product.astype(out.dtype)
        for part in range(parts):
            out[part, at : at + rows, :] = product[part * rows : (part + 1) * rows]

    for third in range(3):

        @pl.when(step == third)
        def gate(third=third):
            spread(dot(hidden[...], gate_up[...], 0, 0), third * shard, shard)

    @pl.when(step == 3)
    def project_out():
        spread(dot(mixed[...], attn[...], 0, 0), 3 * shard, shard)

    @pl.when(step == 4)
    def down():
        spread(dot(act[...], cotangent[...], 0, 0), 4 * shard, shard_down)
        used = 4 * shard + shard_down
        if used < out.shape[1]:
            out[:, used:, :] = jnp.zeros((parts, out.shape[1] - used, width), out.dtype)


def weigh(shard, shard_down, parts, mixed, attn, hidden, gate_up, act, cotangent):
    rows, width = mixed.shape
    whole = lambda step: (0, 0)
    fixed = lambda array: pl.BlockSpec(array.shape, whole)
    deep = 32 * -(-(4 * shard + shard_down) // 32)
    return call(
        functools.partial(weigh_kernel, shard, shard_down),
        (5,),
        [
            fixed(mixed),
            fixed(attn),
            fixed(hidden),
            pl.BlockSpec((rows, width), lambda step: (0, jnp.minimum(step, 2))),
            fixed(act),
            fixed(cotangent),
        ],
        pl.BlockSpec((parts, deep, width), lambda step: (0, 0, 0)),
        shape((parts, deep, width), jnp.bfloat16),
        [],
        2 * rows * parts * deep * width,
        2 * rows * width * 8 + parts * deep * width * 2,
    )(mixed, attn, hidden, gate_up, act, cotangent)


def unpack_kernel(shard, shard_down, place, *refs):
    parts, (out, gate, down, total) = refs[:4], refs[4:]
    rows, width = parts[0].shape
    for distance in range(4):
        at = pl.multiple_of((place[0] ^ distance) * rows, 8)
        total[pl.ds(at, rows), :] = parts[distance][...].astype(jnp.float32)
    for third in range(3):
        gate[:, third * width : (third + 1) * width] = total[third * shard : (third + 1) * shard, :]
    out[...] = total[3 * shard : 4 * shard, :]
    down[...] = total[4 * shard : 4 * shard + shard_down, :]


def unpack(place, shard, shard_down, parts):
    rows, width = parts[0].shape
    whole = lambda step, place: (0, 0)
    sizes = [(shard, width), (shard, 3 * width), (shard_down, width)]
    return pl.pallas_call(
        functools.partial(unpack_kernel, shard, shard_down),
        grid_spec=pltpu.PrefetchScalarGridSpec(
            num_scalar_prefetch=1,
            grid=(1,),
            in_specs=[pl.BlockSpec((rows, width), whole)] * 4,
            out_specs=[pl.BlockSpec(size, whole) for size in sizes],
            scratch_shapes=[pltpu.VMEM((4 * rows, width), jnp.float32)],
        ),
        out_shape=[shape(size, jnp.float32) for size in sizes],
        cost_estimate=pl.CostEstimate(
            flops=rows * width, bytes_accessed=24 * rows * width, transcendentals=0
        ),
        compiler_params=pltpu.CompilerParams(vmem_limit_bytes=VMEM),
    )(place, *parts)


def gradients(groups, refs, cos, sin, head_dim, put):
    sources = {}
    for (kind, first, pairs), ref in zip(groups, refs):
        for pair in range(pairs):
            sources.setdefault((kind, first + pair), []).append((ref, pair))

    def total(kind, pair, lanes):
        return sum(
            ref[:, place * lanes : (place + 1) * lanes].astype(jnp.float32)
            for ref, place in sources[kind, pair]
        )

    for pair in sorted({pair for _, pair in sources}):
        query = total("query", pair, LANES)
        query = query * cos - swap_halves(query, head_dim) * sin
        put(0, pair, query.astype(jnp.bfloat16))
        both = total("keys", pair, 2 * LANES)
        key, value = both[:, :LANES], both[:, LANES:]
        key = key * cos - swap_halves(key, head_dim) * sin
        put(1, pair, key.astype(jnp.bfloat16))
        put(2, pair, value.astype(jnp.bfloat16))


def group_kinds(groups):
    lanes = {"query": LANES, "keys": 2 * LANES}
    return [(kind, first, array.shape[1] // lanes[kind]) for kind, first, array in groups]


def unproject_kernel(head_dim, groups, weight, cosine, sine, *refs):
    own_out, other_out, joined = refs[-3:]
    width = weight.shape[1] // 3
    step = pl.program_id(0)
    half_steps = pl.num_programs(0) // 2

    def put(kind, pair, values):
        at = kind * width + pair * LANES
        joined[:, at : at + LANES] = values

    gradients(groups, refs[:-3], cosine[...], sine[...], head_dim, put)
    result = dot(joined[...], weight[...], 1, 1).astype(own_out.dtype)

    @pl.when(step < half_steps)
    def own():
        own_out[...] = result

    @pl.when(step >= half_steps)
    def other():
        other_out[...] = result


def unproject(weight, cosine, sine, groups, head_dim, after=()):
    rows = cosine.shape[0] // 2
    depth, wide = weight.shape
    block = min(256, rows)
    half_steps = rows // block
    row = lambda columns: pl.BlockSpec((block, columns), lambda step: (step, 0))
    return call(
        functools.partial(unproject_kernel, head_dim, group_kinds(groups)),
        (2 * half_steps,),
        [pl.BlockSpec(weight.shape, lambda step: (0, 0)), row(LANES), row(LANES)]
        + [row(array.shape[1]) for _, _, array in groups],
        [
            pl.BlockSpec((block, depth), lambda step: (jnp.minimum(step, half_steps - 1), 0)),
            pl.BlockSpec((block, depth), lambda step: (jnp.maximum(step - half_steps, 0), 0)),
        ],
        [shape((rows, depth), jnp.bfloat16)] * 2,
        [pltpu.VMEM((block, wide), jnp.bfloat16)],
        4 * rows * weight.size,
        2 * rows * (depth * 4 + wide * 8) + weight.size * 2,
        after=after,
    )(weight, cosine, sine, *[array for _, _, array in groups])


def outer_kernel(chips, head_dim, groups, first, place, hidden, cosine, sine, *refs):
    count = len(groups)
    outs, joined, total = refs[count : count + chips], refs[-2], refs[-1]
    width = joined.shape[1] // 3
    step = pl.program_id(0)

    def put(kind, pair, values):
        at = kind * width + (pair - first) * LANES
        joined[:, at : at + LANES] = values

    gradients(groups, refs[:count], cosine[...], sine[...], head_dim, put)
    share = dot(hidden[...], joined[...], 0, 0)

    @pl.when(step == 0)
    def begin():
        total[...] = share

    @pl.when(step > 0)
    def add():
        total[...] += share

    @pl.when(step == pl.num_programs(0) - 1)
    def finish():
        rows = total.shape[0] // chips
        for distance in range(chips):
            at = pl.multiple_of((place[0] ^ distance) * rows, 16)
            outs[distance][...] = total[pl.ds(at, rows), :].astype(outs[distance].dtype)


def outer(place, chips, hidden, cosine, sine, groups, head_dim, after=()):
    rows, depth = hidden.shape
    kinds = group_kinds(groups)
    found = sorted({first + pair for _, first, pairs in kinds for pair in range(pairs)})
    wide = 3 * LANES * len(found)
    block = min(512, rows)
    part = depth // chips
    row = lambda columns: pl.BlockSpec((block, columns), lambda step, place: (step, 0))
    count = 3 + len(groups)

    def body(place, *refs):
        outer_kernel(
            chips, head_dim, kinds, found[0], place, *refs[:count], *refs[count + len(after) :]
        )

    return pl.pallas_call(
        body,
        grid_spec=pltpu.PrefetchScalarGridSpec(
            num_scalar_prefetch=1,
            grid=(rows // block,),
            in_specs=[row(depth), row(LANES), row(LANES)]
            + [row(array.shape[1]) for _, _, array in groups]
            + [pl.BlockSpec(memory_space=pl.ANY)] * len(after),
            out_specs=[pl.BlockSpec((part, wide), lambda step, place: (0, 0))] * chips,
            scratch_shapes=[
                pltpu.VMEM((block, wide), jnp.bfloat16),
                pltpu.VMEM((depth, wide), jnp.float32),
            ],
        ),
        out_shape=[shape((part, wide), jnp.bfloat16)] * chips,
        cost_estimate=pl.CostEstimate(
            flops=2 * rows * depth * wide,
            bytes_accessed=2 * rows * (depth + 4 * wide) + 2 * depth * wide,
            transcendentals=0,
        ),
        compiler_params=pltpu.CompilerParams(vmem_limit_bytes=VMEM),
    )(place, hidden, cosine, sine, *[array for _, _, array in groups], *after)


def finish_kernel(tokens, near, far, gain, grad_resid, out, gain_out):
    values = tokens[...].astype(jnp.float32)
    centre = values - jnp.mean(values, -1, keepdims=True)
    inverse = lax.rsqrt(jnp.mean(centre * centre, -1, keepdims=True) + norm_eps)
    unit = centre * inverse
    grad_hidden = near[...].astype(jnp.float32) + far[...].astype(jnp.float32)
    share = jnp.sum(grad_hidden * unit, 0, keepdims=True)
    step = pl.program_id(0)

    @pl.when(step == 0)
    def begin():
        gain_out[...] = share

    @pl.when(step > 0)
    def add():
        gain_out[...] += share

    grad_unit = grad_hidden * gain[...]
    grad_norm = inverse * (
        grad_unit
        - jnp.mean(grad_unit, -1, keepdims=True)
        - unit * jnp.mean(grad_unit * unit, -1, keepdims=True)
    )
    out[...] = (grad_resid[...] + grad_norm).astype(out.dtype)


def finish(tokens, near, far, gain, grad_resid, after):
    rows, width = tokens.shape
    block = min(256, rows)
    row = pl.BlockSpec((block, width), lambda step: (step, 0))
    one = pl.BlockSpec((1, width), lambda step: (0, 0))
    return call(
        finish_kernel,
        (rows // block,),
        [row, row, row, one, row],
        [row, one],
        [shape((rows, width), jnp.bfloat16), shape((1, width), jnp.float32)],
        [],
        rows * width * 20,
        rows * width * 12,
        after=after,
    )(tokens, near, far, gain, grad_resid)


EXTRA = 16


def gain_rows(gains, wide):
    rows, width = gains.shape
    blank = jnp.zeros((rows, wide - width), jnp.float32)
    below = jnp.zeros((EXTRA - rows, wide), jnp.float32)
    return jnp.concatenate([jnp.concatenate([gains, blank], 1), below], 0)


def fold_kernel(chips, place, *refs):
    parts, (first, second), outs, total = refs[:chips], refs[chips : chips + 2], refs[-5:-1], refs[-1]
    total[...] = sum(ref[...].astype(jnp.float32) for ref in parts)
    rows, wide = total.shape[0] // 4, total.shape[1]
    extra = gain_rows(jnp.concatenate([first[...], second[...]], 0), wide)
    for distance in range(4):
        at = pl.multiple_of((place[0] ^ distance) * rows, 8)
        outs[distance][:rows, :] = total[pl.ds(at, rows), :].astype(outs[distance].dtype)
        outs[distance][rows:, :] = extra.astype(outs[distance].dtype)


def fold(place, parts, first, second):
    rows, wide = parts[0].shape
    whole = lambda step, place: (0, 0)
    arrays = [*parts, first, second]
    types = [jnp.float32] + [jnp.bfloat16] * 3
    return pl.pallas_call(
        functools.partial(fold_kernel, len(parts)),
        grid_spec=pltpu.PrefetchScalarGridSpec(
            num_scalar_prefetch=1,
            grid=(1,),
            in_specs=[pl.BlockSpec(array.shape, whole) for array in arrays],
            out_specs=[pl.BlockSpec((rows // 4 + EXTRA, wide), whole)] * 4,
            scratch_shapes=[pltpu.VMEM((rows, wide), jnp.float32)],
        ),
        out_shape=[shape((rows // 4 + EXTRA, wide), dtype) for dtype in types],
        cost_estimate=pl.CostEstimate(
            flops=8 * rows * wide, bytes_accessed=10 * rows * wide, transcendentals=0
        ),
        compiler_params=pltpu.CompilerParams(vmem_limit_bytes=VMEM),
    )(place, *arrays)


def add_kernel(extra, *refs):
    parts, outs = refs[:4], refs[4:]
    total = sum(ref[...].astype(jnp.float32) for ref in parts)
    rows = total.shape[0] - extra
    outs[0][...] = total[:rows].astype(jnp.bfloat16)
    if extra:
        outs[1][...] = total[rows:]


def add(arrays, extra=0, after=()):
    rows, wide = arrays[0].shape
    whole = lambda step: (0, 0)
    sizes = [(rows - extra, wide, jnp.bfloat16)] + ([(extra, wide, jnp.float32)] if extra else [])
    return call(
        functools.partial(add_kernel, extra),
        (1,),
        [pl.BlockSpec((rows, wide), whole)] * 4,
        [pl.BlockSpec((count, wide), whole) for count, _, _ in sizes],
        [shape((count, wide), dtype) for count, _, dtype in sizes],
        [],
        4 * rows * wide,
        10 * rows * wide,
        after=after,
    )(*arrays)


def order_kernel(chips, scalars, *refs):
    parts, gains, (kept, given, gain_out, total) = refs[:4], refs[4 : 4 + chips], refs[4 + chips :]
    rows = parts[0].shape[0]
    for distance in range(4):
        at = pl.multiple_of((scalars[0] ^ distance) * rows, 8)
        total[pl.ds(at, rows), :] = parts[distance][...].astype(jnp.float32)
    half = kept.shape[0]
    first_core = scalars[1] == 0
    upper, lower = total[:half, :], total[half:, :]
    kept[...] = jnp.where(first_core, upper, lower)
    given[:half, :] = jnp.where(first_core, lower, upper).astype(jnp.bfloat16)
    share = sum(ref[...] for ref in gains)
    given[half:, :] = share.astype(jnp.bfloat16)
    gain_out[...] = share


def order(scalars, parts, gains, after):
    rows, wide = parts[0].shape
    whole = lambda step, scalars: (0, 0)
    sizes = [
        (2 * rows, jnp.float32),
        (2 * rows + EXTRA, jnp.bfloat16),
        (EXTRA, jnp.float32),
    ]
    count = len(parts) + len(gains)

    def body(scalars, *refs):
        order_kernel(len(gains), scalars, *refs[:count], *refs[count + len(after) :])

    return pl.pallas_call(
        body,
        grid_spec=pltpu.PrefetchScalarGridSpec(
            num_scalar_prefetch=1,
            grid=(1,),
            in_specs=[pl.BlockSpec((rows, wide), whole)] * 4
            + [pl.BlockSpec((EXTRA, wide), whole)] * len(gains)
            + [pl.BlockSpec(memory_space=pl.ANY)] * len(after),
            out_specs=[pl.BlockSpec((count, wide), whole) for count, _ in sizes],
            scratch_shapes=[pltpu.VMEM((4 * rows, wide), jnp.float32)],
        ),
        out_shape=[shape((count, wide), dtype) for count, dtype in sizes],
        cost_estimate=pl.CostEstimate(
            flops=rows * wide, bytes_accessed=24 * rows * wide, transcendentals=0
        ),
        compiler_params=pltpu.CompilerParams(vmem_limit_bytes=VMEM),
    )(scalars, *parts, *gains, *after)


def weave_kernel(scalars, kept, taken, gains, out, gain_out):
    first_core = scalars[0] == 0
    rows = kept.shape[0]
    mine, theirs = kept[...], taken[:rows, :].astype(jnp.float32)
    half = mine.shape[1] // 3
    for third in range(3):
        part = slice(third * half, (third + 1) * half)
        at = 2 * third * half
        out[:, at : at + half] = jnp.where(first_core, mine[:, part], theirs[:, part])
        out[:, at + half : at + 2 * half] = jnp.where(first_core, theirs[:, part], mine[:, part])
    total = (gains[...] + taken[rows:, :].astype(jnp.float32))[:8]
    found = jnp.zeros((8, rows), jnp.float32)
    for device in range(2 * half // rows):
        found = jnp.where(scalars[1] == device, total[:, device * rows : (device + 1) * rows], found)
    gain_out[...] = found


def weave(scalars, kept, taken, gains):
    rows, wide = kept.shape
    arrays = (kept, taken, gains)
    whole = lambda step, scalars: (0, 0)
    return pl.pallas_call(
        weave_kernel,
        grid_spec=pltpu.PrefetchScalarGridSpec(
            num_scalar_prefetch=1,
            grid=(1,),
            in_specs=[pl.BlockSpec(array.shape, whole) for array in arrays],
            out_specs=[pl.BlockSpec((rows, 2 * wide), whole), pl.BlockSpec((8, rows), whole)],
        ),
        out_shape=[shape((rows, 2 * wide), jnp.float32), shape((8, rows), jnp.float32)],
        cost_estimate=pl.CostEstimate(
            flops=rows * wide, bytes_accessed=14 * rows * wide, transcendentals=0
        ),
        compiler_params=pltpu.CompilerParams(vmem_limit_bytes=VMEM),
    )(scalars, *arrays)


def position(axes):
    place = 0
    for axis in axes:
        place = place * lax.axis_size(axis) + lax.axis_index(axis)
    return place


def others(axes):
    count = math.prod(lax.axis_size(axis) for axis in axes)
    return count, [
        [(source, source ^ step) for source in range(count)] for step in range(1, count)
    ]


def exchange(block, axes):
    _, steps = others(axes)
    return [block] + [lax.ppermute(block, axes, pairs) for pairs in steps]


def placed(parts, axes):
    place = position(axes)
    rows = parts[0].shape[0]
    whole = jnp.zeros((len(parts) * rows,) + parts[0].shape[1:], parts[0].dtype)
    for step, part in enumerate(parts):
        whole = lax.dynamic_update_slice_in_dim(whole, part, (place ^ step) * rows, 0)
    return whole


def gather(block, axes):
    if others(axes)[0] > 4:
        return lax.all_gather(block, axes, axis=0, tiled=True)
    return placed(exchange(block, axes), axes)


def receive(parts, axes):
    _, steps = others(axes)
    return [parts[0]] + [
        lax.ppermute(part, axes, pairs) for part, pairs in zip(parts[1:], steps)
    ]


def sum_blocks(parts, axes):
    _, steps = others(axes)
    total = parts[0].astype(jnp.float32)
    for part, pairs in zip(parts[1:], steps):
        total = total + lax.ppermute(part, axes, pairs).astype(jnp.float32)
    return total


def scatter_sum(whole, axes):
    count, _ = others(axes)
    if count > 4:
        return lax.psum_scatter(whole, axes, scatter_dimension=0, tiled=True).astype(jnp.float32)
    place = position(axes)
    rows = whole.shape[0] // count
    return sum_blocks(
        [
            lax.dynamic_slice_in_dim(whole, (place ^ step) * rows, rows, 0)
            for step in range(count)
        ],
        axes,
    )


def full_sum(values, axes):
    count, steps = others(axes)
    if count > 4:
        return lax.psum(values, axes)
    return values + sum(lax.ppermute(values, axes, pairs) for pairs in steps)


def core_swap(block):
    return lax.ppermute(block, "core", [(0, 1), (1, 0)])


def later(arrays, first):
    return lax.optimization_barrier((arrays, first))[0]


def shards(tokens, w_qkv, w_out, w_in, w_down, gain_attn, gain_mlp, lengths, cotangent):
    rows, width = tokens.shape[1:]
    head_dim = width // HEADS
    half = width // 2
    pairs = half // LANES
    chips = lax.axis_size("chip")
    core, inner = lax.axis_index("core"), lax.axis_index("zi")
    first_core = core == 0
    seq_axes, fsdp_axes = ("zp", "zi"), ("chip", "core")
    low = jnp.bfloat16
    few = chips <= 4

    places = [
        (zp, zi, chip, c)
        for zp in range(2)
        for zi in range(2)
        for chip in range(chips)
        for c in range(2)
    ]
    number = {place: index for index, place in enumerate(places)}
    moves = [
        (number[(zp, zi, chip, c)], number[(c, zi, chip, zp)])
        for zp, zi, chip, c in places
        if zp != c
    ]
    stays = lax.axis_index("zp") == core

    def move(array):
        return jnp.where(stays, array, lax.ppermute(array, EVERY, moves))

    swap_chips = [(0, 1), (1, 0)]
    own = move(tokens[0])
    other = core_swap(own)
    far_own = lax.ppermute(own, "zi", swap_chips)

    shard = w_qkv.shape[0]
    pitch = -(-(shard + 1) // 16) * 16
    devices = 2 * chips
    exact = jnp.stack([lengths[0] // 64, lengths[0] % 64]).astype(low)
    filler = jnp.zeros((3 * width - 2 * shard - 2,), low)
    gains = jnp.concatenate([gain_attn, gain_mlp, exact, filler])
    block = jnp.concatenate([w_qkv, jnp.broadcast_to(gains[None], (pitch - shard, 3 * width))], 0)
    raw = lax.all_gather(block, fsdp_axes, axis=0, tiled=True)
    all_gains = raw.reshape(devices, pitch, 3 * width)[:, shard, : 2 * shard + 2].astype(jnp.float32)
    first_gain = all_gains[:, :shard].reshape(1, width)
    second_gain = all_gains[:, shard : 2 * shard].reshape(1, width)
    sequence = 2 * lax.axis_index("chip") + lax.axis_index("zp")
    exact = lax.dynamic_slice_in_dim(all_gains[:, 2 * shard :], sequence, 1, 0)[0]
    length = (exact[0] * 64 + exact[1]).astype(jnp.int32)
    pieces = (devices, pitch, shard)
    if shard % 16:
        raw = raw.reshape(devices, pitch, 3 * width)[:, :shard].reshape(width, 3 * width)
        pieces = (1, width, width)

    w_out, w_in, w_down = later((w_out, w_in, w_down), own)
    m_out = lax.all_gather(w_out, fsdp_axes, axis=0, tiled=True)
    m_in = lax.all_gather(w_in, fsdp_axes, axis=0, tiled=True)
    m_down = lax.all_gather(w_down, fsdp_axes, axis=0, tiled=True)

    steps = jnp.arange(rows)
    own_at = (2 * core + inner) * rows + steps
    other_at = (2 * (1 - core) + inner) * rows + steps
    here = jnp.concatenate([own_at, other_at])
    there = here + jnp.where(inner == 0, rows, -rows)
    run = 64 if rows % 64 == 0 else rows
    cosine, sine = rotary_tables(here[::run], run, head_dim // 2)
    far_cosine, far_sine = rotary_tables(there[::run], run, head_dim // 2)
    near_bias = jnp.where(here < length, 0.0, masked_score).astype(jnp.float32)[None]
    far_bias = jnp.where(there < length, 0.0, masked_score).astype(jnp.float32)[None]

    near, hidden, query, weight = project(
        core[None], own, other, first_gain, raw, cosine, sine, head_dim, pieces
    )
    grad_out = move(later(cotangent[0], near))
    state = attend(query, [(near, near_bias)], last=False)
    far_own = later(far_own, state[1])
    far_other = core_swap(far_own)
    (far,) = project(
        core[None], far_own, far_other, first_gain, weight, far_cosine, far_sine, head_dim,
        after=(state[1],),
    )
    attended, log_total = attend(query, [(far, far_bias)], state)

    theirs = core_swap(attended[rows:])
    (
        mixed,
        layer_out,
        h_second,
        act,
        grad_gate_up,
        grad_resid,
        grad_attn,
        near_back,
        given_back,
        grad_second_gain,
    ) = feed(core[None], own, attended, theirs, m_out, m_in, m_down, second_gain, grad_out)
    layer_out = move(layer_out)
    far_back = core_swap(given_back)

    shard_down = w_down.shape[0]
    if shard % 16 == 0 and shard_down % 16 == 0:
        packed = weigh(
            shard, shard_down, 2 * chips, mixed, grad_attn, h_second, grad_gate_up, act, grad_out
        )
        packed = lax.psum_scatter(packed, fsdp_axes, scatter_dimension=0, tiled=True)[0]
    else:
        grads = (
            dot(h_second, grad_gate_up, 0, 0).reshape(-1, shard, 3, width).transpose(0, 2, 1, 3),
            dot(mixed, grad_attn, 0, 0).reshape(-1, 1, shard, width),
            dot(act, grad_out, 0, 0).reshape(-1, 1, shard_down, width),
        )
        packed = jnp.concatenate(
            [grad.astype(low).reshape(2 * chips, -1, width) for grad in grads], 1
        )
        packed = lax.psum_scatter(packed, fsdp_axes, scatter_dimension=0, tiled=True)[0]

    def back_through(first, count, key_value, bias, after=()):
        return revisit(
            query, first, count, key_value, bias, attended, near_back, far_back, log_total, after=after
        )

    cuts = [(0, pairs - 1), (pairs - 1, 1)]
    tall = few and shard % 16 == 0 and shard_down % 16 == 0
    along = position(seq_axes)
    most = pairs - 1
    far_most = back_through(0, most, far, far_bias)
    far_rest = back_through(most, 1, far, far_bias, (far_most[1],))
    returned = [lax.ppermute(grads[1], "zi", swap_chips) for grads in (far_most, far_rest)]
    near_most = back_through(0, most, near, near_bias, (far_rest[1], layer_out))
    near_rest = back_through(most, 1, near, near_bias, (near_most[1], packed))
    far_grads, near_grads = (far_most, far_rest), (near_most, near_rest)
    after, ready = (), ()
    if tall:
        deep = packed.shape[0] // 4
        quarters = [
            lax.dynamic_slice_in_dim(packed, (along ^ distance) * deep, deep, 0)
            for distance in range(4)
        ]
        (packed,) = add(receive(quarters, seq_axes), after=(near_rest[1],))
        after = (packed,)
        sums = unpack(along[None], shard, shard_down, exchange(packed, seq_axes))
        ready = (sums[0],)
    else:
        packed = lax.psum(packed, seq_axes).astype(jnp.float32)
        total_in = jnp.concatenate([packed[at * shard : (at + 1) * shard] for at in range(3)], 1)
        sums = (packed[3 * shard : 4 * shard], total_in, packed[4 * shard :])
    groups = [
        [
            ("query", first, near_grads[cut][0]),
            ("query", first, far_grads[cut][0]),
            ("keys", first, near_grads[cut][1]),
            ("keys", first, returned[cut]),
        ]
        for cut, first in enumerate((0, most))
    ]
    every = groups[0] + groups[1]

    place = lax.axis_index("chip")
    if tall:
        parts = outer(place[None], chips, hidden, cosine, sine, every, head_dim, after)
        after = (parts[0],)
        parts = receive(parts, ("chip",))
    else:
        (parts,) = outer(place[None] * 0, 1, hidden, cosine, sine, every, head_dim)
        after = ()
    own_hidden, other_hidden = unproject(weight, cosine, sine, every, head_dim, after)
    other_hidden = core_swap(other_hidden)
    grad_tokens, grad_first_gain = finish(
        own, own_hidden, other_hidden, first_gain, grad_resid, (*parts, *ready) if tall else ()
    )
    if tall:
        blocks = fold(along[None], parts, grad_first_gain, grad_second_gain)
        grad_tokens = move(grad_tokens)
        mine, gain_sums = add(receive(blocks, seq_axes), EXTRA)
        gain_sums = exchange(gain_sums, ("chip",))
        kept, given, gain_sums = order(
            jnp.stack([along, core]), exchange(mine, seq_axes), gain_sums, (grad_tokens,)
        )
        total_qkv, gain_sums = weave(
            jnp.stack([core, position(fsdp_axes)]), kept, core_swap(given), gain_sums
        )
    else:
        grad_tokens = move(grad_tokens)
        total = scatter_sum(parts, ("chip",))
        total = scatter_sum(total.astype(low), seq_axes).astype(low)
        total = gather(total, seq_axes)
        kept = jnp.where(first_core, total[:shard], total[shard:])
        given = jnp.where(first_core, total[shard:], total[:shard])
        taken = core_swap(given)
        total_qkv = jnp.where(
            first_core, jnp.stack([kept, taken], 1), jnp.stack([taken, kept], 1)
        ).reshape(shard, 2, 3, half)
        total_qkv = total_qkv.transpose(0, 2, 1, 3).reshape(shard, 3 * width).astype(jnp.float32)

        gain_sums = jnp.concatenate([grad_first_gain, grad_second_gain], 0)
        gain_sums = gain_sums + core_swap(gain_sums)
        gain_sums = full_sum(full_sum(gain_sums, ("chip",)), seq_axes)
        gain_sums = lax.dynamic_slice_in_dim(gain_sums, position(fsdp_axes) * shard, shard, 1)

    return (
        layer_out[None],
        grad_tokens[None],
        total_qkv,
        *sums,
        gain_sums[0],
        gain_sums[1],
    )


def solution(mesh):
    devices = mesh.devices
    split = jax.sharding.Mesh(
        devices.reshape(2, devices.shape[0] // 2, devices.shape[1] // 2, 2), EVERY
    )
    seq, fsdp = ("zp", "zi"), ("chip", "core")
    activation, matrix, vector = P(fsdp, seq, None), P(fsdp, None), P(fsdp)
    return jax.shard_map(
        shards,
        mesh=split,
        in_specs=(activation, matrix, matrix, matrix, matrix, vector, vector, vector, activation),
        out_specs=(activation, activation, matrix, matrix, matrix, matrix, vector, vector),
        check_vma=False,
    )
```

```python
import functools
import math

import jax
import jax.numpy as jnp
from jax import lax
from jax.experimental import pallas as pl
from jax.experimental.pallas import tpu as pltpu
from jax.sharding import PartitionSpec as P

HEADS = 12


norm_eps = 1e-05
rope_base = 160000.0
masked_score = -1e30
LANES = 128
EVERY = ("zp", "zi", "chip", "core")
VMEM = 56 << 20


def dot(left, right, left_dim=1, right_dim=0):
    return lax.dot_general(
        left,
        right,
        (((left_dim,), (right_dim,)), ((), ())),
        preferred_element_type=jnp.float32,
    )


def call(kernel, grid, in_specs, out_specs, out_shape, scratch, flops, moved, exps=0, after=()):
    count, extra = len(in_specs), len(after)

    def body(*refs):
        kernel(*refs[:count], *refs[count + extra :])

    made = pl.pallas_call(
        body,
        grid=grid,
        in_specs=list(in_specs) + [pl.BlockSpec(memory_space=pl.ANY)] * extra,
        out_specs=out_specs,
        out_shape=out_shape,
        scratch_shapes=scratch,
        cost_estimate=pl.CostEstimate(flops=flops, bytes_accessed=moved, transcendentals=exps),
        compiler_params=pltpu.CompilerParams(vmem_limit_bytes=VMEM),
    )
    return lambda *args: made(*args, *after)


def shape(dims, dtype):
    return jax.ShapeDtypeStruct(dims, dtype)


def rotary_tables(starts, steps, half_dim):
    lane = jnp.arange(LANES)
    counter = (lane % half_dim).astype(jnp.float32)
    inverse = jnp.exp(counter * (-math.log(rope_base) / half_dim))
    coarse = (starts.astype(jnp.float32)[:, None] * inverse)[:, None, :]
    fine = (jnp.arange(steps).astype(jnp.float32)[:, None] * inverse)[None]
    cosine = jnp.cos(coarse) * jnp.cos(fine) - jnp.sin(coarse) * jnp.sin(fine)
    sine = jnp.sin(coarse) * jnp.cos(fine) + jnp.cos(coarse) * jnp.sin(fine)
    sign = jnp.where(lane % (2 * half_dim) < half_dim, -1.0, 1.0)
    return cosine.reshape(-1, LANES), (sine * sign).reshape(-1, LANES)


def swap_halves(values, head_dim):
    half = head_dim // 2
    lane = lax.broadcasted_iota(jnp.int32, values.shape, 1)
    ahead = pltpu.roll(values, LANES - half, 1)
    behind = pltpu.roll(values, half, 1)
    return jnp.where(lane % head_dim < half, ahead, behind)


def project_kernel(tiles, head_dim, pieces, core, own, other, gain, cosine, sine, *refs):
    step = pl.program_id(0)
    if pieces:
        raw, (h_out, q_out, weight) = refs[:3], refs[4:]
        count, pitch, shard = pieces
        half = raw[0].shape[1]

        @pl.when(step == 0)
        def compact():
            for piece in range(count):
                for third in range(3):
                    weight[
                        piece * shard : (piece + 1) * shard, third * half : (third + 1) * half
                    ] = raw[third][piece * pitch : piece * pitch + shard, :]

        kv_out = refs[3]
    else:
        weight, kv_out = refs
    values = jnp.where(step < tiles, own[...], other[...]).astype(jnp.float32)
    centre = values - jnp.mean(values, -1, keepdims=True)
    spread = jnp.mean(centre * centre, -1, keepdims=True)
    hidden = (centre * lax.rsqrt(spread + norm_eps) * gain[...]).astype(jnp.bfloat16)
    width = weight.shape[1] // 3
    cos, sin = cosine[...], sine[...]
    if pieces:
        h_out[...] = hidden
        joined = dot(hidden, weight[...])
        start = width
    else:
        joined = dot(hidden, weight[:, width:])
        start = 0
    factor = head_dim ** (-0.5) * math.log2(math.e)
    for pair in range(width // LANES):
        at = pair * LANES
        if pieces:
            query = joined[:, at : at + LANES]
            query = query * cos + swap_halves(query, head_dim) * sin
            q_out[:, at : at + LANES] = (query * factor).astype(jnp.bfloat16)
        key = joined[:, start + at : start + at + LANES]
        key = key * cos + swap_halves(key, head_dim) * sin
        kv_out[:, 2 * at : 2 * at + LANES] = key.astype(jnp.bfloat16)
        value = joined[:, start + width + at : start + width + at + LANES]
        kv_out[:, 2 * at + LANES : 2 * at + 2 * LANES] = value.astype(jnp.bfloat16)


def project(core, own, other, gain, weight, cosine, sine, head_dim, pieces=None, after=()):
    rows, depth = own.shape
    block = min(256, rows)
    tiles = rows // block
    half = depth // 2
    by_row = lambda step, core: (step, 0)
    whole = lambda step, core: (0, 0)
    widths = [2 * half] + ([depth, half] if pieces else [])
    outs = [pl.BlockSpec((block, columns), by_row) for columns in widths]
    shapes = [shape((2 * rows, columns), jnp.bfloat16) for columns in widths]
    if pieces:
        weights = [
            pl.BlockSpec((weight.shape[0], half), lambda step, core, third=third: (0, 2 * third + core[0]))
            for third in range(3)
        ]
        outs.append(pl.BlockSpec((depth, 3 * half), whole))
        shapes.append(shape((depth, 3 * half), jnp.bfloat16))
    else:
        weights = [pl.BlockSpec(weight.shape, whole)]
    count = 5 + len(weights)

    def body(core, *refs):
        project_kernel(tiles, head_dim, pieces, core, *refs[:count], *refs[count + len(after) :])

    return pl.pallas_call(
        body,
        grid_spec=pltpu.PrefetchScalarGridSpec(
            num_scalar_prefetch=1,
            grid=(2 * tiles,),
            in_specs=[
                pl.BlockSpec((block, depth), lambda step, core: (jnp.minimum(step, tiles - 1), 0)),
                pl.BlockSpec((block, depth), lambda step, core: (jnp.maximum(step - tiles, 0), 0)),
                pl.BlockSpec((1, depth), whole),
                pl.BlockSpec((block, LANES), by_row),
                pl.BlockSpec((block, LANES), by_row),
            ]
            + weights
            + [pl.BlockSpec(memory_space=pl.ANY)] * len(after),
            out_specs=outs,
        ),
        out_shape=shapes,
        cost_estimate=pl.CostEstimate(
            flops=2 * 2 * rows * depth * 3 * half,
            bytes_accessed=2 * rows * (2 * depth + 3 * half) * 2 + weight.size * 2,
            transcendentals=0,
        ),
        compiler_params=pltpu.CompilerParams(vmem_limit_bytes=VMEM),
    )(core, own, other, gain, cosine, sine, *[weight] * len(weights), *after)


def attend_kernel(head_dim, sources, first, last, *refs):
    refs = list(refs)
    query = refs.pop(0)
    keys = [(refs.pop(0), refs.pop(0)) for _ in range(sources)]
    if not first:
        acc_in, max_in = refs.pop(0), refs.pop(0)
    if last:
        mixed, log_total = refs.pop(0), refs.pop(0)
    else:
        acc_out, max_out = refs.pop(0), refs.pop(0)
    key_of, value_of, bias_of = refs
    span = keys[0][0].shape[0]

    @pl.when(pl.program_id(1) == 0)
    def prepare():
        low = lax.broadcasted_iota(jnp.int32, (span, LANES), 1) < head_dim
        one = jnp.ones((span, LANES), jnp.bfloat16)
        zero = jnp.zeros((span, LANES), jnp.bfloat16)
        for source, (key_value, bias) in enumerate(keys):
            part = pl.ds(source * span, span)
            key, value = key_value[:, :LANES], key_value[:, LANES:]
            key_of[0, part, :] = jnp.where(low, key, zero)
            key_of[1, part, :] = jnp.where(low, zero, key)
            value_of[0, part, :] = jnp.where(low, value, one)
            value_of[1, part, :] = jnp.where(low, one, value)
            bias_of[:, part] = bias[...]

    rows = query.shape[0]
    block = min(512, rows)
    low = lax.broadcasted_iota(jnp.int32, (block, LANES), 1) < head_dim
    for start in range(0, rows, block):
        part = pl.ds(start, block)
        held = query[part, :]
        results, tops = [], []
        for head in range(2):
            score = dot(held, key_of[head], 1, 1) + bias_of[...]
            top = jnp.max(score, 1, keepdims=True)
            if not first:
                before = max_in[part, head * head_dim : head * head_dim + 1]
                top = jnp.maximum(top, before)
            expo = jnp.exp2(score - top).astype(jnp.bfloat16)
            result = dot(expo, value_of[head])
            if not first:
                kept = acc_in[part, head * LANES : (head + 1) * LANES]
                result = result + kept * jnp.exp2(before - top)
            results.append(result)
            tops.append(top)
        top = jnp.where(low, tops[0], tops[1])
        if last:
            total = jnp.where(
                low, pltpu.roll(results[0], head_dim, 1), pltpu.roll(results[1], head_dim, 1)
            )
            mixed[part, :] = (jnp.where(low, results[0], results[1]) / total).astype(mixed.dtype)
            log_total[part, :] = top + jnp.log2(total)
        else:
            acc_out[part, :LANES] = results[0]
            acc_out[part, LANES:] = results[1]
            max_out[part, :] = top


def attend(query, keys, state=None, last=True, head_dim=64, after=()):
    rows, width = query.shape
    span = keys[0][0].shape[0]
    pairs = width // LANES
    block = rows
    narrow = pl.BlockSpec((block, LANES), lambda pair, step: (step, pair))
    wide = pl.BlockSpec((block, 2 * LANES), lambda pair, step: (step, pair))
    in_specs = [narrow]
    args = [query]
    for key_value, bias in keys:
        in_specs += [
            pl.BlockSpec((span, 2 * LANES), lambda pair, step: (0, pair)),
            pl.BlockSpec((1, span), lambda pair, step: (0, 0)),
        ]
        args += [key_value, bias]
    if state is not None:
        in_specs += [wide, narrow]
        args += list(state)
    if last:
        out_specs = [narrow, narrow]
        out_shape = [shape((rows, width), jnp.bfloat16), shape((rows, width), jnp.float32)]
    else:
        out_specs = [wide, narrow]
        out_shape = [shape((rows, 2 * width), jnp.float32), shape((rows, width), jnp.float32)]
    count = span * len(keys)
    return call(
        functools.partial(attend_kernel, head_dim, len(keys), state is None, last),
        (pairs, rows // block),
        in_specs,
        out_specs,
        out_shape,
        [
            pltpu.VMEM((2, count, LANES), jnp.bfloat16),
            pltpu.VMEM((2, count, LANES), jnp.bfloat16),
            pltpu.VMEM((1, count), jnp.float32),
        ],
        pairs * 2 * 2 * 2 * rows * count * 256,
        pairs * (rows * LANES * 8 + count * 512),
        pairs * 2 * rows * count,
        after,
    )(*args)


def revisit_kernel(
    head_dim, key_value, bias, query, mixed, near_grad, far_grad, log_total,
    dq_out, dkv_out, grad_key, grad_value, key_of, value_of,
):
    span = key_value.shape[0]
    step = pl.program_id(1)

    @pl.when(step == 0)
    def prepare():
        low = lax.broadcasted_iota(jnp.int32, (span, LANES), 1) < head_dim
        zero = jnp.zeros((span, LANES), jnp.bfloat16)
        key, value = key_value[:, :LANES], key_value[:, LANES:]
        key_of[0] = jnp.where(low, key, zero)
        key_of[1] = jnp.where(low, zero, key)
        value_of[0] = jnp.where(low, value, zero)
        value_of[1] = jnp.where(low, zero, value)
        grad_key[...] = jnp.zeros_like(grad_key)
        grad_value[...] = jnp.zeros_like(grad_value)

    rows = query.shape[0]
    block = min(256, rows // 2)
    for start in range(0, rows, block):
        part = pl.ds(start, block)
        held = query[part, :]
        if start < rows // 2:
            back = near_grad[part, :]
        else:
            back = far_grad[pl.ds(start - rows // 2, block), :]
        held_t, back_t = held.T, back.T
        product = back.astype(jnp.float32) * mixed[part, :].astype(jnp.float32)
        grad_query = None
        for head in range(2):
            lanes = slice(head * head_dim, (head + 1) * head_dim)
            weighted = jnp.sum(product[:, lanes], 1, keepdims=True)
            log_block = log_total[part, head * head_dim : head * head_dim + 1]
            prob = jnp.exp2(dot(held, key_of[head], 1, 1) + bias[...] - log_block)
            grad_prob = dot(back, value_of[head], 1, 1)
            grad_score = (prob * (grad_prob - weighted)).astype(jnp.bfloat16)
            grad_value[lanes, :] += dot(back_t[lanes], prob.astype(jnp.bfloat16))
            grad_key[lanes, :] += dot(held_t[lanes], grad_score)
            term = dot(grad_score, key_of[head])
            grad_query = term if grad_query is None else grad_query + term
        dq_out[part, :] = grad_query * head_dim ** (-0.5)

    @pl.when(step == pl.num_programs(1) - 1)
    def finish():
        dkv_out[:, :LANES] = (grad_key[...].T * math.log(2.0)).astype(dkv_out.dtype)
        dkv_out[:, LANES:] = grad_value[...].T.astype(dkv_out.dtype)


def revisit(
    query, first, pairs, key_value, bias, mixed, near_grad, far_grad, log_total, head_dim=64, after=()
):
    rows = query.shape[0]
    span = key_value.shape[0]
    of_all = pl.BlockSpec((rows, LANES), lambda pair, step: (0, first + pair))
    half_of_all = pl.BlockSpec((rows // 2, LANES), lambda pair, step: (0, first + pair))
    narrow = pl.BlockSpec((rows, LANES), lambda pair, step: (0, pair))
    return call(
        functools.partial(revisit_kernel, head_dim),
        (pairs, 1),
        [
            pl.BlockSpec((span, 2 * LANES), lambda pair, step: (0, first + pair)),
            pl.BlockSpec((1, span), lambda pair, step: (0, 0)),
            of_all,
            of_all,
            half_of_all,
            half_of_all,
            of_all,
        ],
        [narrow, pl.BlockSpec((span, 2 * LANES), lambda pair, step: (0, pair))],
        [
            shape((rows, pairs * LANES), jnp.float32),
            shape((span, pairs * 2 * LANES), jnp.bfloat16),
        ],
        [
            pltpu.VMEM((LANES, span), jnp.float32),
            pltpu.VMEM((LANES, span), jnp.float32),
            pltpu.VMEM((2, span, LANES), jnp.bfloat16),
            pltpu.VMEM((2, span, LANES), jnp.bfloat16),
        ],
        pairs * 5 * 2 * 2 * rows * span * 200,
        pairs * (rows * LANES * 14 + span * 1024),
        pairs * 2 * rows * span,
        after,
    )(key_value, bias, query, mixed, near_grad, far_grad, log_total)


def feed_kernel(
    core, tokens, mine, theirs, m_out, m_in, m_down, gain, cotangent,
    mixed_out, layer_out, hidden_out, act_out, gate_up_out, resid_out, attn_out, kept_out, given_out,
    gain_out,
):
    width_ff = m_down.shape[0]
    half = theirs.shape[1]
    first_core = core[0] == 0
    near, far = mine[...], theirs[...]
    left = jnp.where(first_core, near, far)
    right = jnp.where(first_core, far, near)
    mixed_out[:, :half] = left
    mixed_out[:, half:] = right
    resid = tokens[...].astype(jnp.float32) + dot(mixed_out[...], m_out[...])
    centre = resid - jnp.mean(resid, -1, keepdims=True)
    inverse = lax.rsqrt(jnp.mean(centre * centre, -1, keepdims=True) + norm_eps)
    unit = centre * inverse
    hidden = (unit * gain[...]).astype(jnp.bfloat16)
    hidden_out[...] = hidden
    gate_up = dot(hidden, m_in[...])
    gate, upper = gate_up[:, :width_ff], gate_up[:, width_ff:]
    phi = 0.5 * (1.0 + lax.erf(gate * math.sqrt(0.5)))
    gelu = gate * phi
    slope = phi + gate * (jnp.exp(-0.5 * gate * gate) * (1.0 / math.sqrt(2.0 * math.pi)))
    act = (gelu * upper).astype(jnp.bfloat16)
    act_out[...] = act
    layer_out[...] = (resid + dot(act, m_down[...])).astype(layer_out.dtype)
    back = cotangent[...]
    grad_act = dot(back, m_down[...], 1, 1)
    gate_up_out[:, :width_ff] = (grad_act * upper * slope).astype(jnp.bfloat16)
    gate_up_out[:, width_ff:] = (grad_act * gelu).astype(jnp.bfloat16)
    grad_hidden = dot(gate_up_out[...], m_in[...], 1, 1)
    share = jnp.sum(grad_hidden * unit, 0, keepdims=True)
    step = pl.program_id(0)

    @pl.when(step == 0)
    def begin():
        gain_out[...] = share

    @pl.when(step > 0)
    def add():
        gain_out[...] += share

    grad_unit = grad_hidden * gain[...]
    grad_resid = back.astype(jnp.float32) + inverse * (
        grad_unit
        - jnp.mean(grad_unit, -1, keepdims=True)
        - unit * jnp.mean(grad_unit * unit, -1, keepdims=True)
    )
    resid_out[...] = grad_resid
    grad_attn = grad_resid.astype(jnp.bfloat16)
    attn_out[...] = grad_attn
    grad_mixed = dot(grad_attn, m_out[...], 1, 1).astype(jnp.bfloat16)
    left, right = grad_mixed[:, :half], grad_mixed[:, half:]
    kept_out[...] = jnp.where(first_core, left, right)
    given_out[...] = jnp.where(first_core, right, left)


def feed(core, tokens, mine, theirs, m_out, m_in, m_down, gain, cotangent):
    rows, width = tokens.shape
    half = width // 2
    block = min(256, rows)
    by_row = lambda step, core: (step, 0)
    whole = lambda step, core: (0, 0)
    row = lambda columns: pl.BlockSpec((block, columns), by_row)
    fixed = lambda array: pl.BlockSpec(array.shape, whole, pipeline_mode=pl.Buffered(1))
    columns = [
        (width, jnp.bfloat16),
        (width, jnp.bfloat16),
        (width, jnp.bfloat16),
        (m_down.shape[0], jnp.bfloat16),
        (m_in.shape[1], jnp.bfloat16),
        (width, jnp.float32),
        (width, jnp.bfloat16),
        (half, jnp.bfloat16),
        (half, jnp.bfloat16),
    ]
    return pl.pallas_call(
        feed_kernel,
        grid_spec=pltpu.PrefetchScalarGridSpec(
            num_scalar_prefetch=1,
            grid=(rows // block,),
            in_specs=[
                row(width),
                row(half),
                row(half),
                fixed(m_out),
                fixed(m_in),
                fixed(m_down),
                pl.BlockSpec((1, width), whole),
                row(width),
            ],
            out_specs=[row(count) for count, _ in columns] + [pl.BlockSpec((1, width), whole)],
        ),
        out_shape=[shape((rows, count), dtype) for count, dtype in columns]
        + [shape((1, width), jnp.float32)],
        cost_estimate=pl.CostEstimate(
            flops=4 * rows * (m_out.size + m_in.size + m_down.size),
            bytes_accessed=2 * (m_out.size + m_in.size + m_down.size) + rows * width * 30,
            transcendentals=2 * rows * m_down.shape[0],
        ),
        compiler_params=pltpu.CompilerParams(vmem_limit_bytes=VMEM),
    )(core, tokens, mine, theirs, m_out, m_in, m_down, gain, cotangent)


def weigh_kernel(shard, shard_down, mixed, attn, hidden, gate_up, act, cotangent, out):
    step = pl.program_id(0)
    width = mixed.shape[1]
    parts = out.shape[0]

    def spread(product, at, rows):
        product = product.astype(out.dtype)
        for part in range(parts):
            out[part, at : at + rows, :] = product[part * rows : (part + 1) * rows]

    for third in range(3):

        @pl.when(step == third)
        def gate(third=third):
            spread(dot(hidden[...], gate_up[...], 0, 0), third * shard, shard)

    @pl.when(step == 3)
    def project_out():
        spread(dot(mixed[...], attn[...], 0, 0), 3 * shard, shard)

    @pl.when(step == 4)
    def down():
        spread(dot(act[...], cotangent[...], 0, 0), 4 * shard, shard_down)
        used = 4 * shard + shard_down
        if used < out.shape[1]:
            out[:, used:, :] = jnp.zeros((parts, out.shape[1] - used, width), out.dtype)


def weigh(shard, shard_down, parts, mixed, attn, hidden, gate_up, act, cotangent):
    rows, width = mixed.shape
    whole = lambda step: (0, 0)
    fixed = lambda array: pl.BlockSpec(array.shape, whole)
    deep = 32 * -(-(4 * shard + shard_down) // 32)
    return call(
        functools.partial(weigh_kernel, shard, shard_down),
        (5,),
        [
            fixed(mixed),
            fixed(attn),
            fixed(hidden),
            pl.BlockSpec((rows, width), lambda step: (0, jnp.minimum(step, 2))),
            fixed(act),
            fixed(cotangent),
        ],
        pl.BlockSpec((parts, deep, width), lambda step: (0, 0, 0)),
        shape((parts, deep, width), jnp.bfloat16),
        [],
        2 * rows * parts * deep * width,
        2 * rows * width * 8 + parts * deep * width * 2,
    )(mixed, attn, hidden, gate_up, act, cotangent)


def unpack_kernel(shard, shard_down, place, *refs):
    parts, (out, gate, down, total) = refs[:4], refs[4:]
    rows, width = parts[0].shape
    for distance in range(4):
        at = pl.multiple_of((place[0] ^ distance) * rows, 8)
        total[pl.ds(at, rows), :] = parts[distance][...].astype(jnp.float32)
    for third in range(3):
        gate[:, third * width : (third + 1) * width] = total[third * shard : (third + 1) * shard, :]
    out[...] = total[3 * shard : 4 * shard, :]
    down[...] = total[4 * shard : 4 * shard + shard_down, :]


def unpack(place, shard, shard_down, parts):
    rows, width = parts[0].shape
    whole = lambda step, place: (0, 0)
    sizes = [(shard, width), (shard, 3 * width), (shard_down, width)]
    return pl.pallas_call(
        functools.partial(unpack_kernel, shard, shard_down),
        grid_spec=pltpu.PrefetchScalarGridSpec(
            num_scalar_prefetch=1,
            grid=(1,),
            in_specs=[pl.BlockSpec((rows, width), whole)] * 4,
            out_specs=[pl.BlockSpec(size, whole) for size in sizes],
            scratch_shapes=[pltpu.VMEM((4 * rows, width), jnp.float32)],
        ),
        out_shape=[shape(size, jnp.float32) for size in sizes],
        cost_estimate=pl.CostEstimate(
            flops=rows * width, bytes_accessed=24 * rows * width, transcendentals=0
        ),
        compiler_params=pltpu.CompilerParams(vmem_limit_bytes=VMEM),
    )(place, *parts)


def gradients(groups, refs, cos, sin, head_dim, put):
    sources = {}
    for (kind, first, pairs), ref in zip(groups, refs):
        for pair in range(pairs):
            sources.setdefault((kind, first + pair), []).append((ref, pair))

    def total(kind, pair, lanes):
        return sum(
            ref[:, place * lanes : (place + 1) * lanes].astype(jnp.float32)
            for ref, place in sources[kind, pair]
        )

    for pair in sorted({pair for _, pair in sources}):
        query = total("query", pair, LANES)
        query = query * cos - swap_halves(query, head_dim) * sin
        put(0, pair, query.astype(jnp.bfloat16))
        both = total("keys", pair, 2 * LANES)
        key, value = both[:, :LANES], both[:, LANES:]
        key = key * cos - swap_halves(key, head_dim) * sin
        put(1, pair, key.astype(jnp.bfloat16))
        put(2, pair, value.astype(jnp.bfloat16))


def group_kinds(groups):
    lanes = {"query": LANES, "keys": 2 * LANES}
    return [(kind, first, array.shape[1] // lanes[kind]) for kind, first, array in groups]


def unproject_kernel(head_dim, groups, weight, cosine, sine, *refs):
    own_out, other_out, joined = refs[-3:]
    width = weight.shape[1] // 3
    step = pl.program_id(0)
    half_steps = pl.num_programs(0) // 2

    def put(kind, pair, values):
        at = kind * width + pair * LANES
        joined[:, at : at + LANES] = values

    gradients(groups, refs[:-3], cosine[...], sine[...], head_dim, put)
    result = dot(joined[...], weight[...], 1, 1).astype(own_out.dtype)

    @pl.when(step < half_steps)
    def own():
        own_out[...] = result

    @pl.when(step >= half_steps)
    def other():
        other_out[...] = result


def unproject(weight, cosine, sine, groups, head_dim, after=()):
    rows = cosine.shape[0] // 2
    depth, wide = weight.shape
    block = min(256, rows)
    half_steps = rows // block
    row = lambda columns: pl.BlockSpec((block, columns), lambda step: (step, 0))
    return call(
        functools.partial(unproject_kernel, head_dim, group_kinds(groups)),
        (2 * half_steps,),
        [pl.BlockSpec(weight.shape, lambda step: (0, 0)), row(LANES), row(LANES)]
        + [row(array.shape[1]) for _, _, array in groups],
        [
            pl.BlockSpec((block, depth), lambda step: (jnp.minimum(step, half_steps - 1), 0)),
            pl.BlockSpec((block, depth), lambda step: (jnp.maximum(step - half_steps, 0), 0)),
        ],
        [shape((rows, depth), jnp.bfloat16)] * 2,
        [pltpu.VMEM((block, wide), jnp.bfloat16)],
        4 * rows * weight.size,
        2 * rows * (depth * 4 + wide * 8) + weight.size * 2,
        after=after,
    )(weight, cosine, sine, *[array for _, _, array in groups])


def outer_kernel(chips, head_dim, groups, first, place, hidden, cosine, sine, *refs):
    count = len(groups)
    outs, joined, total = refs[count : count + chips], refs[-2], refs[-1]
    width = joined.shape[1] // 3
    step = pl.program_id(0)

    def put(kind, pair, values):
        at = kind * width + (pair - first) * LANES
        joined[:, at : at + LANES] = values

    gradients(groups, refs[:count], cosine[...], sine[...], head_dim, put)
    share = dot(hidden[...], joined[...], 0, 0)

    @pl.when(step == 0)
    def begin():
        total[...] = share

    @pl.when(step > 0)
    def add():
        total[...] += share

    @pl.when(step == pl.num_programs(0) - 1)
    def finish():
        rows = total.shape[0] // chips
        for distance in range(chips):
            at = pl.multiple_of((place[0] ^ distance) * rows, 16)
            outs[distance][...] = total[pl.ds(at, rows), :].astype(outs[distance].dtype)


def outer(place, chips, hidden, cosine, sine, groups, head_dim, after=()):
    rows, depth = hidden.shape
    kinds = group_kinds(groups)
    found = sorted({first + pair for _, first, pairs in kinds for pair in range(pairs)})
    wide = 3 * LANES * len(found)
    block = min(512, rows)
    part = depth // chips
    row = lambda columns: pl.BlockSpec((block, columns), lambda step, place: (step, 0))
    count = 3 + len(groups)

    def body(place, *refs):
        outer_kernel(
            chips, head_dim, kinds, found[0], place, *refs[:count], *refs[count + len(after) :]
        )

    return pl.pallas_call(
        body,
        grid_spec=pltpu.PrefetchScalarGridSpec(
            num_scalar_prefetch=1,
            grid=(rows // block,),
            in_specs=[row(depth), row(LANES), row(LANES)]
            + [row(array.shape[1]) for _, _, array in groups]
            + [pl.BlockSpec(memory_space=pl.ANY)] * len(after),
            out_specs=[pl.BlockSpec((part, wide), lambda step, place: (0, 0))] * chips,
            scratch_shapes=[
                pltpu.VMEM((block, wide), jnp.bfloat16),
                pltpu.VMEM((depth, wide), jnp.float32),
            ],
        ),
        out_shape=[shape((part, wide), jnp.bfloat16)] * chips,
        cost_estimate=pl.CostEstimate(
            flops=2 * rows * depth * wide,
            bytes_accessed=2 * rows * (depth + 4 * wide) + 2 * depth * wide,
            transcendentals=0,
        ),
        compiler_params=pltpu.CompilerParams(vmem_limit_bytes=VMEM),
    )(place, hidden, cosine, sine, *[array for _, _, array in groups], *after)


def finish_kernel(tokens, near, far, gain, grad_resid, out, gain_out):
    values = tokens[...].astype(jnp.float32)
    centre = values - jnp.mean(values, -1, keepdims=True)
    inverse = lax.rsqrt(jnp.mean(centre * centre, -1, keepdims=True) + norm_eps)
    unit = centre * inverse
    grad_hidden = near[...].astype(jnp.float32) + far[...].astype(jnp.float32)
    share = jnp.sum(grad_hidden * unit, 0, keepdims=True)
    step = pl.program_id(0)

    @pl.when(step == 0)
    def begin():
        gain_out[...] = share

    @pl.when(step > 0)
    def add():
        gain_out[...] += share

    grad_unit = grad_hidden * gain[...]
    grad_norm = inverse * (
        grad_unit
        - jnp.mean(grad_unit, -1, keepdims=True)
        - unit * jnp.mean(grad_unit * unit, -1, keepdims=True)
    )
    out[...] = (grad_resid[...] + grad_norm).astype(out.dtype)


def finish(tokens, near, far, gain, grad_resid, after):
    rows, width = tokens.shape
    block = min(256, rows)
    row = pl.BlockSpec((block, width), lambda step: (step, 0))
    one = pl.BlockSpec((1, width), lambda step: (0, 0))
    return call(
        finish_kernel,
        (rows // block,),
        [row, row, row, one, row],
        [row, one],
        [shape((rows, width), jnp.bfloat16), shape((1, width), jnp.float32)],
        [],
        rows * width * 20,
        rows * width * 12,
        after=after,
    )(tokens, near, far, gain, grad_resid)


EXTRA = 16


def gain_rows(gains, wide):
    rows, width = gains.shape
    blank = jnp.zeros((rows, wide - width), jnp.float32)
    below = jnp.zeros((EXTRA - rows, wide), jnp.float32)
    return jnp.concatenate([jnp.concatenate([gains, blank], 1), below], 0)


def fold_kernel(chips, place, *refs):
    parts, (first, second), outs, total = refs[:chips], refs[chips : chips + 2], refs[-5:-1], refs[-1]
    total[...] = sum(ref[...].astype(jnp.float32) for ref in parts)
    rows, wide = total.shape[0] // 4, total.shape[1]
    extra = gain_rows(jnp.concatenate([first[...], second[...]], 0), wide)
    for distance in range(4):
        at = pl.multiple_of((place[0] ^ distance) * rows, 8)
        outs[distance][:rows, :] = total[pl.ds(at, rows), :].astype(outs[distance].dtype)
        outs[distance][rows:, :] = extra.astype(outs[distance].dtype)


def fold(place, parts, first, second):
    rows, wide = parts[0].shape
    whole = lambda step, place: (0, 0)
    arrays = [*parts, first, second]
    types = [jnp.float32] + [jnp.bfloat16] * 3
    return pl.pallas_call(
        functools.partial(fold_kernel, len(parts)),
        grid_spec=pltpu.PrefetchScalarGridSpec(
            num_scalar_prefetch=1,
            grid=(1,),
            in_specs=[pl.BlockSpec(array.shape, whole) for array in arrays],
            out_specs=[pl.BlockSpec((rows // 4 + EXTRA, wide), whole)] * 4,
            scratch_shapes=[pltpu.VMEM((rows, wide), jnp.float32)],
        ),
        out_shape=[shape((rows // 4 + EXTRA, wide), dtype) for dtype in types],
        cost_estimate=pl.CostEstimate(
            flops=8 * rows * wide, bytes_accessed=10 * rows * wide, transcendentals=0
        ),
        compiler_params=pltpu.CompilerParams(vmem_limit_bytes=VMEM),
    )(place, *arrays)


def add_kernel(extra, *refs):
    parts, outs = refs[:4], refs[4:]
    total = sum(ref[...].astype(jnp.float32) for ref in parts)
    rows = total.shape[0] - extra
    outs[0][...] = total[:rows].astype(jnp.bfloat16)
    if extra:
        outs[1][...] = total[rows:]


def add(arrays, extra=0, after=()):
    rows, wide = arrays[0].shape
    whole = lambda step: (0, 0)
    sizes = [(rows - extra, wide, jnp.bfloat16)] + ([(extra, wide, jnp.float32)] if extra else [])
    return call(
        functools.partial(add_kernel, extra),
        (1,),
        [pl.BlockSpec((rows, wide), whole)] * 4,
        [pl.BlockSpec((count, wide), whole) for count, _, _ in sizes],
        [shape((count, wide), dtype) for count, _, dtype in sizes],
        [],
        4 * rows * wide,
        10 * rows * wide,
        after=after,
    )(*arrays)


def order_kernel(chips, scalars, *refs):
    parts, gains, (kept, given, gain_out, total) = refs[:4], refs[4 : 4 + chips], refs[4 + chips :]
    rows = parts[0].shape[0]
    for distance in range(4):
        at = pl.multiple_of((scalars[0] ^ distance) * rows, 8)
        total[pl.ds(at, rows), :] = parts[distance][...].astype(jnp.float32)
    half = kept.shape[0]
    first_core = scalars[1] == 0
    upper, lower = total[:half, :], total[half:, :]
    kept[...] = jnp.where(first_core, upper, lower)
    given[:half, :] = jnp.where(first_core, lower, upper).astype(jnp.bfloat16)
    share = sum(ref[...] for ref in gains)
    given[half:, :] = share.astype(jnp.bfloat16)
    gain_out[...] = share


def order(scalars, parts, gains, after):
    rows, wide = parts[0].shape
    whole = lambda step, scalars: (0, 0)
    sizes = [
        (2 * rows, jnp.float32),
        (2 * rows + EXTRA, jnp.bfloat16),
        (EXTRA, jnp.float32),
    ]
    count = len(parts) + len(gains)

    def body(scalars, *refs):
        order_kernel(len(gains), scalars, *refs[:count], *refs[count + len(after) :])

    return pl.pallas_call(
        body,
        grid_spec=pltpu.PrefetchScalarGridSpec(
            num_scalar_prefetch=1,
            grid=(1,),
            in_specs=[pl.BlockSpec((rows, wide), whole)] * 4
            + [pl.BlockSpec((EXTRA, wide), whole)] * len(gains)
            + [pl.BlockSpec(memory_space=pl.ANY)] * len(after),
            out_specs=[pl.BlockSpec((count, wide), whole) for count, _ in sizes],
            scratch_shapes=[pltpu.VMEM((4 * rows, wide), jnp.float32)],
        ),
        out_shape=[shape((count, wide), dtype) for count, dtype in sizes],
        cost_estimate=pl.CostEstimate(
            flops=rows * wide, bytes_accessed=24 * rows * wide, transcendentals=0
        ),
        compiler_params=pltpu.CompilerParams(vmem_limit_bytes=VMEM),
    )(scalars, *parts, *gains, *after)


def weave_kernel(scalars, kept, taken, gains, out, gain_out):
    first_core = scalars[0] == 0
    rows = kept.shape[0]
    mine, theirs = kept[...], taken[:rows, :].astype(jnp.float32)
    half = mine.shape[1] // 3
    for third in range(3):
        part = slice(third * half, (third + 1) * half)
        at = 2 * third * half
        out[:, at : at + half] = jnp.where(first_core, mine[:, part], theirs[:, part])
        out[:, at + half : at + 2 * half] = jnp.where(first_core, theirs[:, part], mine[:, part])
    total = (gains[...] + taken[rows:, :].astype(jnp.float32))[:8]
    found = jnp.zeros((8, rows), jnp.float32)
    for device in range(2 * half // rows):
        found = jnp.where(scalars[1] == device, total[:, device * rows : (device + 1) * rows], found)
    gain_out[...] = found


def weave(scalars, kept, taken, gains):
    rows, wide = kept.shape
    arrays = (kept, taken, gains)
    whole = lambda step, scalars: (0, 0)
    return pl.pallas_call(
        weave_kernel,
        grid_spec=pltpu.PrefetchScalarGridSpec(
            num_scalar_prefetch=1,
            grid=(1,),
            in_specs=[pl.BlockSpec(array.shape, whole) for array in arrays],
            out_specs=[pl.BlockSpec((rows, 2 * wide), whole), pl.BlockSpec((8, rows), whole)],
        ),
        out_shape=[shape((rows, 2 * wide), jnp.float32), shape((8, rows), jnp.float32)],
        cost_estimate=pl.CostEstimate(
            flops=rows * wide, bytes_accessed=14 * rows * wide, transcendentals=0
        ),
        compiler_params=pltpu.CompilerParams(vmem_limit_bytes=VMEM),
    )(scalars, *arrays)


def position(axes):
    place = 0
    for axis in axes:
        place = place * lax.axis_size(axis) + lax.axis_index(axis)
    return place


def others(axes):
    count = math.prod(lax.axis_size(axis) for axis in axes)
    return count, [
        [(source, source ^ step) for source in range(count)] for step in range(1, count)
    ]


def exchange(block, axes):
    _, steps = others(axes)
    return [block] + [lax.ppermute(block, axes, pairs) for pairs in steps]


def placed(parts, axes):
    place = position(axes)
    rows = parts[0].shape[0]
    whole = jnp.zeros((len(parts) * rows,) + parts[0].shape[1:], parts[0].dtype)
    for step, part in enumerate(parts):
        whole = lax.dynamic_update_slice_in_dim(whole, part, (place ^ step) * rows, 0)
    return whole


def gather(block, axes):
    if others(axes)[0] > 4:
        return lax.all_gather(block, axes, axis=0, tiled=True)
    return placed(exchange(block, axes), axes)


def receive(parts, axes):
    _, steps = others(axes)
    return [parts[0]] + [
        lax.ppermute(part, axes, pairs) for part, pairs in zip(parts[1:], steps)
    ]


def sum_blocks(parts, axes):
    _, steps = others(axes)
    total = parts[0].astype(jnp.float32)
    for part, pairs in zip(parts[1:], steps):
        total = total + lax.ppermute(part, axes, pairs).astype(jnp.float32)
    return total


def scatter_sum(whole, axes):
    count, _ = others(axes)
    if count > 4:
        return lax.psum_scatter(whole, axes, scatter_dimension=0, tiled=True).astype(jnp.float32)
    place = position(axes)
    rows = whole.shape[0] // count
    return sum_blocks(
        [
            lax.dynamic_slice_in_dim(whole, (place ^ step) * rows, rows, 0)
            for step in range(count)
        ],
        axes,
    )


def full_sum(values, axes):
    count, steps = others(axes)
    if count > 4:
        return lax.psum(values, axes)
    return values + sum(lax.ppermute(values, axes, pairs) for pairs in steps)


def core_swap(block):
    return lax.ppermute(block, "core", [(0, 1), (1, 0)])


def later(arrays, first):
    return lax.optimization_barrier((arrays, first))[0]


def shards(tokens, w_qkv, w_out, w_in, w_down, gain_attn, gain_mlp, lengths, cotangent):
    rows, width = tokens.shape[1:]
    head_dim = width // HEADS
    half = width // 2
    pairs = half // LANES
    chips = lax.axis_size("chip")
    core, inner = lax.axis_index("core"), lax.axis_index("zi")
    first_core = core == 0
    seq_axes, fsdp_axes = ("zp", "zi"), ("chip", "core")
    low = jnp.bfloat16
    few = chips <= 4

    places = [
        (zp, zi, chip, c)
        for zp in range(2)
        for zi in range(2)
        for chip in range(chips)
        for c in range(2)
    ]
    number = {place: index for index, place in enumerate(places)}
    moves = [
        (number[(zp, zi, chip, c)], number[(c, zi, chip, zp)])
        for zp, zi, chip, c in places
        if zp != c
    ]
    stays = lax.axis_index("zp") == core

    def move(array):
        return jnp.where(stays, array, lax.ppermute(array, EVERY, moves))

    swap_chips = [(0, 1), (1, 0)]
    own = move(tokens[0])
    other = core_swap(own)
    far_own = lax.ppermute(own, "zi", swap_chips)

    shard = w_qkv.shape[0]
    pitch = -(-(shard + 1) // 16) * 16
    devices = 2 * chips
    exact = jnp.stack([lengths[0] // 64, lengths[0] % 64]).astype(low)
    filler = jnp.zeros((3 * width - 2 * shard - 2,), low)
    gains = jnp.concatenate([gain_attn, gain_mlp, exact, filler])
    block = jnp.concatenate([w_qkv, jnp.broadcast_to(gains[None], (pitch - shard, 3 * width))], 0)
    raw = lax.all_gather(block, fsdp_axes, axis=0, tiled=True)
    all_gains = raw.reshape(devices, pitch, 3 * width)[:, shard, : 2 * shard + 2].astype(jnp.float32)
    first_gain = all_gains[:, :shard].reshape(1, width)
    second_gain = all_gains[:, shard : 2 * shard].reshape(1, width)
    sequence = 2 * lax.axis_index("chip") + lax.axis_index("zp")
    exact = lax.dynamic_slice_in_dim(all_gains[:, 2 * shard :], sequence, 1, 0)[0]
    length = (exact[0] * 64 + exact[1]).astype(jnp.int32)
    pieces = (devices, pitch, shard)
    if shard % 16:
        raw = raw.reshape(devices, pitch, 3 * width)[:, :shard].reshape(width, 3 * width)
        pieces = (1, width, width)

    w_out, w_in, w_down = later((w_out, w_in, w_down), own)
    m_out = lax.all_gather(w_out, fsdp_axes, axis=0, tiled=True)
    m_in = lax.all_gather(w_in, fsdp_axes, axis=0, tiled=True)
    m_down = lax.all_gather(w_down, fsdp_axes, axis=0, tiled=True)

    steps = jnp.arange(rows)
    own_at = (2 * core + inner) * rows + steps
    other_at = (2 * (1 - core) + inner) * rows + steps
    here = jnp.concatenate([own_at, other_at])
    there = here + jnp.where(inner == 0, rows, -rows)
    run = 64 if rows % 64 == 0 else rows
    cosine, sine = rotary_tables(here[::run], run, head_dim // 2)
    far_cosine, far_sine = rotary_tables(there[::run], run, head_dim // 2)
    near_bias = jnp.where(here < length, 0.0, masked_score).astype(jnp.float32)[None]
    far_bias = jnp.where(there < length, 0.0, masked_score).astype(jnp.float32)[None]

    near, hidden, query, weight = project(
        core[None], own, other, first_gain, raw, cosine, sine, head_dim, pieces
    )
    grad_out = move(later(cotangent[0], near))
    state = attend(query, [(near, near_bias)], last=False)
    far_own = later(far_own, state[1])
    far_other = core_swap(far_own)
    (far,) = project(
        core[None], far_own, far_other, first_gain, weight, far_cosine, far_sine, head_dim,
        after=(state[1],),
    )
    attended, log_total = attend(query, [(far, far_bias)], state)

    theirs = core_swap(attended[rows:])
    (
        mixed,
        layer_out,
        h_second,
        act,
        grad_gate_up,
        grad_resid,
        grad_attn,
        near_back,
        given_back,
        grad_second_gain,
    ) = feed(core[None], own, attended, theirs, m_out, m_in, m_down, second_gain, grad_out)
    layer_out = move(layer_out)
    far_back = core_swap(given_back)

    shard_down = w_down.shape[0]
    if shard % 16 == 0 and shard_down % 16 == 0:
        packed = weigh(
            shard, shard_down, 2 * chips, mixed, grad_attn, h_second, grad_gate_up, act, grad_out
        )
        packed = lax.psum_scatter(packed, fsdp_axes, scatter_dimension=0, tiled=True)[0]
    else:
        grads = (
            dot(h_second, grad_gate_up, 0, 0).reshape(-1, shard, 3, width).transpose(0, 2, 1, 3),
            dot(mixed, grad_attn, 0, 0).reshape(-1, 1, shard, width),
            dot(act, grad_out, 0, 0).reshape(-1, 1, shard_down, width),
        )
        packed = jnp.concatenate(
            [grad.astype(low).reshape(2 * chips, -1, width) for grad in grads], 1
        )
        packed = lax.psum_scatter(packed, fsdp_axes, scatter_dimension=0, tiled=True)[0]

    def back_through(first, count, key_value, bias, after=()):
        return revisit(
            query, first, count, key_value, bias, attended, near_back, far_back, log_total, after=after
        )

    cuts = [(0, pairs - 1), (pairs - 1, 1)]
    tall = few and shard % 16 == 0 and shard_down % 16 == 0
    along = position(seq_axes)
    most = pairs - 1
    far_most = back_through(0, most, far, far_bias)
    far_rest = back_through(most, 1, far, far_bias, (far_most[1],))
    returned = [lax.ppermute(grads[1], "zi", swap_chips) for grads in (far_most, far_rest)]
    near_most = back_through(0, most, near, near_bias, (far_rest[1], layer_out))
    near_rest = back_through(most, 1, near, near_bias, (near_most[1], packed))
    far_grads, near_grads = (far_most, far_rest), (near_most, near_rest)
    after, ready = (), ()
    if tall:
        deep = packed.shape[0] // 4
        quarters = [
            lax.dynamic_slice_in_dim(packed, (along ^ distance) * deep, deep, 0)
            for distance in range(4)
        ]
        (packed,) = add(receive(quarters, seq_axes), after=(near_rest[1],))
        after = (packed,)
        sums = unpack(along[None], shard, shard_down, exchange(packed, seq_axes))
        ready = (sums[0],)
    else:
        packed = lax.psum(packed, seq_axes).astype(jnp.float32)
        total_in = jnp.concatenate([packed[at * shard : (at + 1) * shard] for at in range(3)], 1)
        sums = (packed[3 * shard : 4 * shard], total_in, packed[4 * shard :])
    groups = [
        [
            ("query", first, near_grads[cut][0]),
            ("query", first, far_grads[cut][0]),
            ("keys", first, near_grads[cut][1]),
            ("keys", first, returned[cut]),
        ]
        for cut, first in enumerate((0, most))
    ]
    every = groups[0] + groups[1]

    place = lax.axis_index("chip")
    if tall:
        parts = outer(place[None], chips, hidden, cosine, sine, every, head_dim, after)
        after = (parts[0],)
        parts = receive(parts, ("chip",))
    else:
        (parts,) = outer(place[None] * 0, 1, hidden, cosine, sine, every, head_dim)
        after = ()
    own_hidden, other_hidden = unproject(weight, cosine, sine, every, head_dim, (*after, *ready))
    other_hidden = core_swap(other_hidden)
    grad_tokens, grad_first_gain = finish(
        own, own_hidden, other_hidden, first_gain, grad_resid, ()
    )
    if tall:
        blocks = fold(along[None], parts, grad_first_gain, grad_second_gain)
        grad_tokens = move(grad_tokens)
        mine, gain_sums = add(receive(blocks, seq_axes), EXTRA)
        gain_sums = exchange(gain_sums, ("chip",))
        kept, given, gain_sums = order(
            jnp.stack([along, core]), exchange(mine, seq_axes), gain_sums, (grad_tokens,)
        )
        total_qkv, gain_sums = weave(
            jnp.stack([core, position(fsdp_axes)]), kept, core_swap(given), gain_sums
        )
    else:
        grad_tokens = move(grad_tokens)
        total = scatter_sum(parts, ("chip",))
        total = scatter_sum(total.astype(low), seq_axes).astype(low)
        total = gather(total, seq_axes)
        kept = jnp.where(first_core, total[:shard], total[shard:])
        given = jnp.where(first_core, total[shard:], total[:shard])
        taken = core_swap(given)
        total_qkv = jnp.where(
            first_core, jnp.stack([kept, taken], 1), jnp.stack([taken, kept], 1)
        ).reshape(shard, 2, 3, half)
        total_qkv = total_qkv.transpose(0, 2, 1, 3).reshape(shard, 3 * width).astype(jnp.float32)

        gain_sums = jnp.concatenate([grad_first_gain, grad_second_gain], 0)
        gain_sums = gain_sums + core_swap(gain_sums)
        gain_sums = full_sum(full_sum(gain_sums, ("chip",)), seq_axes)
        gain_sums = lax.dynamic_slice_in_dim(gain_sums, position(fsdp_axes) * shard, shard, 1)

    return (
        layer_out[None],
        grad_tokens[None],
        total_qkv,
        *sums,
        gain_sums[0],
        gain_sums[1],
    )


def solution(mesh):
    devices = mesh.devices
    split = jax.sharding.Mesh(
        devices.reshape(2, devices.shape[0] // 2, devices.shape[1] // 2, 2), EVERY
    )
    seq, fsdp = ("zp", "zi"), ("chip", "core")
    activation, matrix, vector = P(fsdp, seq, None), P(fsdp, None), P(fsdp)
    return jax.shard_map(
        shards,
        mesh=split,
        in_specs=(activation, matrix, matrix, matrix, matrix, vector, vector, vector, activation),
        out_specs=(activation, activation, matrix, matrix, matrix, matrix, vector, vector),
        check_vma=False,
    )
```
